128 devices in a mesh: user: 32 (over y, z, core), ctx: 4 (over x).
Axes of the slice: x: 4, y: 4, z: 4, core: 2. Of those that a mesh axis runs over, the one named last changes fastest.
Arguments:
- owner: int32 [32, 2048, 1], P('user', 'ctx'), may hold values from 0 to 127; in each aligned block of 512 rows (0 to 511, 512 to 1023, ..., all dimensions but the last counted through in order) at most 8 rows name the same one
- row: int32 [32, 2048], P('user', 'ctx'), may hold values from 0 to 2047
- lengths: int32 [32], P('user'), may hold values from 512 to 2048, as said below
- table: bfloat16 [262144, 512], P(('user', 'ctx')), may hold values from -36 to 36
- proj_weight: bfloat16 [512, 2048], replicated, may hold values from -0.25 to 0.25
- out_weight: bfloat16 [512, 512], replicated, may hold values from -0.25 to 0.25
- out_grad: bfloat16 [32, 2048, 512], P('user', 'ctx'), may hold values from -6 to 6
Outputs:
- mixed: bfloat16 [32, 2048, 512], P('user', 'ctx')
- table_grad: float32 [262144, 512], P(('user', 'ctx'))
The draws below stay inside these ranges and needn't reach their ends.
Inputs may be any that keep to these rules, and one draw needn't show every extreme that they name: Among the events of one device (aligned blocks of 512 positions of one user) no owner is named more than 8 times, a bound that some block reaches. `lengths`: one user's history fills all 2048 positions and another's holds exactly 512 events.
All inputs are finite; a program needn't handle non-finite values.
Results may differ from the reference program's by a relative error of at most 0.007.
Values may be sent and summed in bfloat16 or wider, within the bound.
A program may use at most 128 MiB of HBM per device.

```python
import math
import jax
import jax.numpy as jnp
import numpy as np
from jax import lax

D = 512
HEADS = 4
HEAD_DIM = 128
TOK_DEV = 512
ROWS_DEV = 2048
SEQ = 2048
TABLE_ROWS = 262144
CAP = 8
N_USER = 32
N_CTX = 4


def draw_lengths(key, part):
    key = jax.random.fold_in(key, 5)
    first_key, second_key, third_key = jax.random.split(key, 3)
    spread = jax.random.randint(first_key, (N_USER,), SEQ // 4, SEQ + 1)
    longest = jax.random.randint(second_key, (), 0, N_USER)
    shortest = (longest + 1 + jax.random.randint(third_key, (), 0, N_USER - 1)) % N_USER
    places = jnp.arange(N_USER)
    chosen = jnp.where(places == longest, SEQ, jnp.where(places == shortest, SEQ // 4, spread))
    return chosen.astype(jnp.int32)


def draw_table(key, part):
    key = jax.random.fold_in(key, 9)
    row_key, column_key, base_key = jax.random.split(key, 3)
    row_scale = jnp.exp(jax.random.uniform(row_key, (TABLE_ROWS, 1), jnp.float32, math.log(0.3), math.log(3.0)))
    column_scale = jnp.exp(jax.random.uniform(column_key, (1, D), jnp.float32, math.log(0.3), math.log(3.0)))
    base = jnp.clip(jax.random.normal(base_key, (TABLE_ROWS, D), jnp.float32), -4.0, 4.0)
    return (base * row_scale * column_scale).astype(jnp.bfloat16)


def set_ends(entries, stream_key, low, top_value):
    place = [jax.random.randint(jax.random.fold_in(stream_key, axis), (), 0, length) for axis, length in enumerate(entries.shape)]
    widest = entries.shape.index(max(entries.shape))
    neighbour = place[:widest] + [(place[widest] + 1) % entries.shape[widest]] + place[widest + 1:]
    return entries.at[tuple(place)].set(low).at[tuple(neighbour)].set(top_value)


def block_scale(own_key, dims, pieces, smallest, high):
    level = 1.0
    for position, parts in pieces:
        heights = jax.random.uniform(jax.random.fold_in(jax.random.fold_in(own_key, 6), position), (parts,), jnp.float32, smallest / len(pieces), high / len(pieces))
        level = level * jnp.repeat(jnp.exp(heights), dims[position] // parts).reshape((-1,) + (1,) * (len(dims) - 1 - position))
    return level


def shared_out(own_key, own, number, rows, count, top, most, lean):
    sequence = jax.random.permutation(own_key, count)
    crowded, usual = portions_of(count, rows * top, most, lean, True), portions_of(count, rows * top, most, lean, False)
    places = jnp.arange(count)

    def named(sizes, rotation):
        used = int((sizes > 0).sum())
        fixed = max(1, used // 4)
        shifted = fixed + (places - fixed + rotation * (used - fixed)) % max(1, count - fixed)
        return jnp.zeros((count,), jnp.int32).at[sequence[jnp.where(places < fixed, places, shifted)]].set(jnp.asarray(sizes, jnp.int32))

    sizes = jnp.where(number % 4 == 0, named(crowded, number // 4), named(usual, number - number // 4 - 1))
    mixed = jax.random.permutation(jax.random.fold_in(own, 3), count)
    donor, sink = mixed[0:count // 2 * 2:2], mixed[1:count // 2 * 2:2]
    room = jnp.minimum(sizes[donor] - 1, most - sizes[sink]) // 2
    room = jnp.where((donor == sequence[0]) | (sink == sequence[0]) | (sizes[sink] == 0), 0, jnp.maximum(room, 0))
    shifted = jax.random.randint(jax.random.fold_in(own, 4), (count // 2,), 0, 1 << 20) % (room + 1)
    sizes = sizes.at[donor].add(-shifted).at[sink].add(shifted)
    labels = jnp.searchsorted(jnp.cumsum(sizes), jnp.arange(rows * top), side="right").astype(jnp.int32)
    grid = labels.reshape(top, rows).T
    grid = grid[jax.random.permutation(jax.random.fold_in(own, 1), rows)]
    rotation = jax.random.randint(jax.random.fold_in(own, 2), (rows, 1), 0, top)
    return jnp.take_along_axis(grid, (jnp.arange(top)[None, :] + rotation) % top, axis=1)


def portions_of(number_of, total, limit, skew, full):
    loads = [(1 << 20) // math.isqrt(standing ** skew) + 1 for standing in range(1, number_of + 1)]
    largest = limit if full else min(limit, max(-(-total // number_of), total * loads[0] // sum(loads)))
    least = 1 if total - largest >= number_of - 1 else 0
    holding, rest = [largest] + [least] * (number_of - 1), total - largest - least * (number_of - 1)
    while rest > 0:
        candidates = [i for i in range(1, number_of) if holding[i] < largest] or [i for i in range(1, number_of) if holding[i] < limit]
        mass, budget = sum([loads[i] for i in candidates]), rest
        for i in candidates:
            more = min(limit - holding[i], max(1, budget * loads[i] // mass), rest)
            holding[i] = holding[i] + more
            rest = rest - more
    return np.array(holding)


def gaussian(stream_key, extent, width, most, shards=(), kind=jnp.bfloat16):
    loudness = block_scale(stream_key, extent, shards, -0.22, 0.18) if shards else 1.0
    drawn = jax.random.normal(stream_key, extent, jnp.float32) * width * loudness
    return jnp.minimum(jnp.maximum(drawn, -most), most).astype(kind)


def setup_inputs(seed: int = 0) -> dict:
    seeds = jax.random.split(jax.random.key(seed), 8)
    owner_keys = jax.random.split(jax.random.fold_in(seeds[0], 1), N_USER * SEQ // TOK_DEV)
    owner_turns = jax.random.permutation(jax.random.fold_in(seeds[0], 3), N_USER * SEQ // TOK_DEV)
    owner = jax.vmap(lambda own, number: shared_out(jax.random.fold_in(seeds[0], 2), own, number, TOK_DEV, N_USER * N_CTX, 1, CAP, 1))(owner_keys, owner_turns).reshape((N_USER, SEQ, 1))
    row = set_ends(jax.random.randint(seeds[1], (N_USER, SEQ), 0, ROWS_DEV), jax.random.fold_in(seeds[1], 1), 0, ROWS_DEV - 1).astype(jnp.int32)
    lengths = draw_lengths(jax.random.fold_in(seeds[7], 71), 0)
    table = draw_table(jax.random.fold_in(seeds[7], 71), 0)
    proj_weight = gaussian(seeds[4], (D, 4 * D), D ** -0.5, 0.25)
    out_weight = gaussian(seeds[5], (D, D), D ** -0.5, 0.25)
    out_grad = gaussian(seeds[6], (N_USER, SEQ, D), 1.0, 6.0, ((0, 32), (1, 4)))
    return {"owner": owner, "row": row, "lengths": lengths, "table": table, "proj_weight": proj_weight, "out_weight": out_weight, "out_grad": out_grad}


EPSILON = 1e-05

def normalize(values):
    center = lax.optimization_barrier(jnp.mean(values, -1, keepdims=True))
    deviation = values - center
    inverse = lax.rsqrt(lax.optimization_barrier(jnp.mean(deviation * deviation, -1, keepdims=True)) + EPSILON)
    return (deviation * inverse, inverse)

def norm_back(incoming, normed, inverse):
    return inverse * (incoming - lax.optimization_barrier(jnp.mean(incoming, -1, keepdims=True)) - normed * lax.optimization_barrier(jnp.mean(incoming * normed, -1, keepdims=True)))

def silu_slope(values):
    sigma = jax.nn.sigmoid(values)
    return sigma * (1.0 + values * (1.0 - sigma))

def rounded(values):
    return lax.optimization_barrier(values.astype(jnp.bfloat16)).astype(jnp.float32)

def user_layer(rows_in, grad_in, length, proj_weight, out_weight):
    places = jnp.arange(SEQ, dtype=jnp.int32)
    in_history = (places < length)[:, None]
    embed = rows_in.astype(jnp.float32)
    normed, embed_scale = normalize(embed)
    projected = jnp.dot(normed.astype(jnp.bfloat16), proj_weight, preferred_element_type=jnp.float32)
    activated = rounded(jax.nn.silu(projected))
    gate_u = activated[:, :D]
    query = activated[:, D:2 * D].reshape(SEQ, HEADS, HEAD_DIM)
    keys = activated[:, 2 * D:3 * D].reshape(SEQ, HEADS, HEAD_DIM)
    values = activated[:, 3 * D:].reshape(SEQ, HEADS, HEAD_DIM)
    scores = jnp.einsum('qhd,khd->hqk', query, keys) * HEAD_DIM ** (-0.5)
    allowed = ((places[None, :] <= places[:, None]) & (places[None, :] < length))[None]
    weights = rounded(jnp.where(allowed, jax.nn.silu(scores), 0.0))
    attended = jnp.einsum('hqk,khd->qhd', weights, values).reshape(SEQ, D)
    attn_norm, attn_scale = normalize(attended)
    gated = (attn_norm * gate_u).astype(jnp.bfloat16)
    output = jnp.dot(gated, out_weight, preferred_element_type=jnp.float32)
    mixed = jnp.where(in_history, embed + output, 0.0).astype(jnp.bfloat16)
    masked = jnp.where(in_history, grad_in, jnp.zeros_like(grad_in))
    gated_grad = jnp.dot(masked, out_weight.T, preferred_element_type=jnp.float32)
    gate_grad = gated_grad * attn_norm
    attn_grad = rounded(norm_back(gated_grad * gate_u, attn_norm, attn_scale)).reshape(SEQ, HEADS, HEAD_DIM)
    slope = jnp.einsum('qhd,khd->hqk', attn_grad, values)
    score_grad = rounded(jnp.where(allowed, slope * silu_slope(scores) * HEAD_DIM ** (-0.5), 0.0))
    value_grad = jnp.einsum('hqk,qhd->khd', weights, attn_grad).reshape(SEQ, D)
    query_grad = jnp.einsum('hqk,khd->qhd', score_grad, keys).reshape(SEQ, D)
    key_grad = jnp.einsum('hqk,qhd->khd', score_grad, query).reshape(SEQ, D)
    joined = jnp.concatenate([gate_grad, query_grad, key_grad, value_grad], 1)
    proj_grad = (joined * silu_slope(projected)).astype(jnp.bfloat16)
    embed_in = jnp.dot(proj_grad, proj_weight.T, preferred_element_type=jnp.float32)
    embed_grad = norm_back(embed_in, normed, embed_scale) + masked.astype(jnp.float32)
    return (mixed, embed_grad)

def reference(owner, row, lengths, table, proj_weight, out_weight, out_grad):
    item_ids = (owner[..., 0] * ROWS_DEV + row).astype(jnp.int32)
    embedded = jnp.take(table, item_ids.reshape(-1), axis=0).reshape(N_USER, SEQ, D)

    def one_user(packed):
        return user_layer(packed[0], packed[1], packed[2], proj_weight, out_weight)
    mixed, embed_grad = lax.map(one_user, (embedded, out_grad, lengths))
    table_grad = jnp.zeros((TABLE_ROWS, D), jnp.float32).at[item_ids.reshape(-1)].add(embed_grad.reshape(-1, D))
    return (mixed, table_grad)
```

```python
import jax
import jax.numpy as jnp
from jax import lax
from jax.experimental import pallas as pl
from jax.experimental.pallas import tpu as pltpu
from jax.sharding import PartitionSpec as P

MESH = pl.DeviceIdType.MESH
F32 = jnp.float32
BF16 = jnp.bfloat16
NC = 4
ND = 128
TOK = 512
SEQ = 2048
D = 512
HD = 128
CAP = 8
ROWS = 2048
SLOTS = ND * CAP
GROUP = 32
EPSILON = 1e-05
SCALE = HD ** (-0.5)
QT = 256


def div(a, b):
    return lax.div(a, jnp.int32(b))


def rem(a, b):
    return lax.rem(a, jnp.int32(b))


def swapped(flat):
    core = rem(div(flat, 4), 2)
    x, y, z = rem(flat, 4), div(flat, 32), rem(div(flat, 8), 4)
    other = ((x * 4 + z) * 2 + core) * 4 + y
    return flat + core * (other - flat)


def place(flat):
    return (div(flat, NC), rem(flat, NC))


def iota(shape, axis):
    return lax.broadcasted_iota(jnp.int32, shape, axis)


def to_column(line):
    n = line.shape[1]
    eye = iota((n, n), 0) == iota((n, n), 1)
    return jnp.sum(jnp.where(eye, line, 0.0), axis=1, keepdims=True)


def to_line(column):
    n = column.shape[0]
    eye = iota((n, n), 0) == iota((n, n), 1)
    return jnp.sum(jnp.where(eye, column, 0.0), axis=0, keepdims=True)


def one_hot(match):
    return jnp.where(match, 1.0, 0.0).astype(BF16)


def dot(a, b, ca=1, cb=0):
    return lax.dot_general(a, b, (((ca,), (cb,)), ((), ())), preferred_element_type=F32)


def remote(src, dst, send, recv, target):
    return pltpu.make_async_remote_copy(
        src_ref=src, dst_ref=dst, send_sem=send, recv_sem=recv, device_id=target, device_id_type=MESH
    )


def tile_of(q, k):
    return div(q * (q + 1), 2) + k


def settle(view, sem):
    pltpu.make_async_copy(view, view, sem).wait()


def layer(
    owner, row, length, table_h, pw_h, ow_h, og_h,
    mixed, recv2, wrow,
    table, pw, ow, og, og_in, wh, vbuf, vall, out1, recv1, x_all, emb, normed, r_x,
    q_s, k_s, v_s, g_s, slopes, gg_send, gg, att, w_t, d_t, d_att, dq_s, gated_s, dg_s, dk_s, dv_s, dqo_s,
    gated_r, pg, mix, stats, out2, d_kv,
    load, ids_s, ids_r, og_s, og_r, a_s, a_r, gg_ss, gg_rs, x_ss, x_rs, st_s, st_r, ex_s, ex_r, mx_s, mx_r, b_s, b_r,
):
    user, ctx = lax.axis_index("user"), lax.axis_index("ctx")
    me = user * NC + ctx
    core = rem(user, 2)
    held = swapped(me)
    block = rem(held, NC)
    away = held != me

    def peer(j):
        z = rem(div(user, 2), 4)
        other = (j * 4 + z) * 2 + 1
        return (user + core * (other - user), j + core * (ctx - j))

    def each_peer(k):
        return rem(block + k, NC)

    barrier = pltpu.get_barrier_semaphore()

    def greet(k, carry):
        pl.semaphore_signal(barrier, inc=1, device_id=place(rem(me + k, ND)), device_id_type=MESH)
        return carry

    lax.fori_loop(1, ND, greet, 0)

    head = pl.multiple_of(block * HD, HD)
    loads = [
        pltpu.make_async_copy(og_h, og_in, load.at[0]),
        pltpu.make_async_copy(table_h, table, load.at[1]),
        pltpu.make_async_copy(ow_h, ow, load.at[2]),
        pltpu.make_async_copy(pw_h, pw, load.at[3]),
    ]
    for copy in loads:
        copy.start()

    places = ctx * TOK + iota((1, TOK), 1)
    valid = places < length[0]
    own = jnp.where(valid, owner[...], -1)
    match = iota((ND, TOK), 0) == own
    before = one_hot(iota((TOK, TOK), 0) < iota((TOK, TOK), 1))
    rank = dot(one_hot(match), before)
    slot = jnp.sum(jnp.where(match, rank, 0.0), axis=0, keepdims=True).astype(jnp.int32)
    packed = jnp.where(valid, (own * CAP + slot) * ROWS + row[...], -1)
    vbuf[0] = packed
    vall[me] = packed

    pl.semaphore_wait(barrier, ND - 1)

    def tell(k, carry):
        remote(vbuf.at[0], vall.at[me], ids_s, ids_r, place(rem(me + k, ND))).start()
        return carry

    lax.fori_loop(1, ND, tell, 0)
    loads[0].wait()

    @pl.when(away)
    def _():
        remote(og_in, og, og_s, og_r, place(held)).start()

    settle(vall.at[pl.ds(0, ND - 1)], ids_r)
    loads[1].wait()

    def answer(step, carry):
        group = rem(step + div(me, GROUP), ND // GROUP)
        first = pl.multiple_of(group * GROUP, GROUP)
        asked = vall[pl.ds(first, GROUP)]
        mine = (lax.shift_right_arithmetic(asked, 11) - me * CAP) == iota((GROUP, CAP, 1), 1)
        wanted = jnp.where(mine, (jnp.bitwise_and(asked, ROWS - 1) + 1).astype(F32), 0.0)
        wanted = (jnp.sum(wanted, axis=2, keepdims=True) - 1.0).reshape(GROUP * CAP, 1)
        wrow[:, pl.ds(pl.multiple_of(group * GROUP * CAP, GROUP * CAP), GROUP * CAP)] = to_line(wanted)
        found = dot(one_hot(iota((GROUP * CAP, ROWS), 1) == wanted.astype(jnp.int32)), table[...])
        halves = [found[:, :256].reshape(GROUP, CAP, 256), found[:, 256:].reshape(GROUP, CAP, 256)]
        out1[pl.ds(first, GROUP)] = jnp.concatenate(halves, axis=1).astype(BF16)

        def send(k, inner):
            source = first + rem(k + me, GROUP)
            target = swapped(source)

            @pl.when(target != me)
            def _():
                remote(out1.at[source], recv1.at[me], a_s, a_r, place(target)).start()

            @pl.when(target == me)
            def _():
                recv1[me] = out1[source]

            return inner

        lax.fori_loop(0, GROUP, send, 0)
        return carry

    lax.fori_loop(0, ND // GROUP, answer, 0)

    slot_line = lax.shift_right_arithmetic(vall[held], 11).astype(F32)
    slot_col = to_column(slot_line)
    inside = slot_col >= 0.0
    loads[2].wait()
    loads[3].wait()

    @pl.when(away)
    def _():
        settle(og, og_r)

    @pl.when(jnp.logical_not(away))
    def _():
        og[...] = og_in[...]

    masked = jnp.where(inside, og[...], jnp.zeros((TOK, D), BF16))
    og[...] = masked
    gated_grad = dot(masked, ow[...], 1, 1).astype(BF16)
    for j in range(NC):
        gg_send[j] = gated_grad[:, j * HD:(j + 1) * HD]
    for k in range(1, NC):
        j = each_peer(k)
        remote(gg_send.at[j], gg.at[block], gg_ss, gg_rs, peer(j)).start()
    gg[block] = gg_send[block]
    for part in range(4):
        wh[:, part * HD:(part + 1) * HD] = pw[:, pl.ds(pl.multiple_of(part * D + head, HD), HD)]

    settle(recv1.at[pl.ds(0, ND - 1)], a_r)
    embed = jnp.zeros((TOK, D), F32)
    for g in range(ND // GROUP):
        got = recv1[g * GROUP:(g + 1) * GROUP].astype(F32)
        rows = jnp.concatenate(
            [got[:, :CAP].reshape(GROUP * CAP, 256), got[:, CAP:].reshape(GROUP * CAP, 256)], axis=1
        ).astype(BF16)
        lanes = iota((TOK, GROUP * CAP), 1) + g * GROUP * CAP
        embed = embed + dot(one_hot(lanes == slot_col.astype(jnp.int32)), rows)
    emb[...] = embed.astype(BF16)
    center = jnp.mean(embed, -1, keepdims=True)
    deviation = embed - center
    inverse = lax.rsqrt(jnp.mean(deviation * deviation, -1, keepdims=True) + EPSILON)
    norm = deviation * inverse
    normed[...] = norm
    r_x[...] = inverse
    x_all[block] = norm.astype(BF16)
    for k in range(1, NC):
        remote(x_all.at[block], x_all.at[block], x_ss.at[k], x_rs.at[k], peer(each_peer(k))).start()

    def project(j):
        for half in range(2):
            projected = dot(x_all[j, half * 256:(half + 1) * 256], wh[...])
            sigma = jax.nn.sigmoid(projected)
            silu = projected * sigma
            where = pl.ds(pl.multiple_of(j * TOK + half * 256, 256), 256)
            slopes[where, :] = sigma + silu * (1.0 - sigma)
            low = silu.astype(BF16)
            g_s[where, :] = low[:, :HD]
            q_s[where, :] = low[:, HD:2 * HD]
            k_s[where, :] = low[:, 2 * HD:3 * HD]
            v_s[where, :] = low[:, 3 * HD:]

    project(block)
    for k in range(1, NC):
        settle(x_all.at[0], x_rs.at[k])
        project(rem(block - k + NC, NC))
    settle(gg.at[pl.ds(0, 3)], gg_rs)

    def forward(qb, carry):
        rows = pl.ds(pl.multiple_of(qb * QT, QT), QT)
        query = q_s[rows, :]

        def tile(kb, total):
            cols = pl.ds(pl.multiple_of(kb * TOK, TOK), TOK)
            scores = dot(query, k_s[cols, :], 1, 1) * SCALE
            allowed = (iota((QT, TOK), 1) - iota((QT, TOK), 0)) <= (qb * QT - kb * TOK)
            sigma = jax.nn.sigmoid(scores)
            silu = scores * sigma
            weights = jnp.where(allowed, silu, 0.0).astype(BF16)
            place_t = tile_of(div(qb, 2), kb)
            half = pl.ds(pl.multiple_of(rem(qb, 2) * QT, QT), QT)
            w_t[place_t, half, :] = weights
            d_t[place_t, half, :] = jnp.where(allowed, (sigma + silu * (1.0 - sigma)) * SCALE, 0.0)
            return total + dot(weights, v_s[cols, :])

        total = lax.fori_loop(0, div(qb, 2) + 1, tile, jnp.zeros((QT, HD), F32))
        att[rows, :] = total
        gate = g_s[rows, :].astype(F32)
        incoming = gg[div(qb, 2), pl.ds(pl.multiple_of(rem(qb, 2) * QT, QT), QT), :].astype(F32)
        cot = incoming * gate
        mean = jnp.mean(total, -1, keepdims=True)
        off = total - mean
        spread = jnp.sum(off * off, -1, keepdims=True)
        c_sum = jnp.sum(cot, -1, keepdims=True)
        c_off = jnp.sum(cot * off, -1, keepdims=True)
        lane = iota((QT, HD), 1)
        table4 = jnp.where(lane == 0, mean, jnp.where(lane == 1, spread, jnp.where(lane == 2, c_sum, c_off)))
        stats[block, :, rows] = table4.T[:8]
        return carry

    lax.fori_loop(0, SEQ // QT, forward, 0)
    for k in range(1, NC):
        remote(stats.at[block], stats.at[block], st_s, st_r, peer(each_peer(k))).start()
    settle(stats.at[pl.ds(0, 3)], st_r)

    means = [stats[h, 0:1, :] for h in range(NC)]
    mean = (means[0] + means[1] + means[2] + means[3]) * (1.0 / NC)
    spread = 0.0
    c_sum = 0.0
    c_off = 0.0
    for h in range(NC):
        gap = means[h] - mean
        spread = spread + stats[h, 1:2, :] + HD * gap * gap
        c_sum = c_sum + stats[h, 2:3, :]
        c_off = c_off + stats[h, 3:4, :] + stats[h, 2:3, :] * gap
    r_a = lax.rsqrt(spread * (1.0 / D) + EPSILON)
    c_mean = c_sum * (1.0 / D)
    c_norm = r_a * c_off * (1.0 / D)
    sub = iota((8, SEQ), 0)
    rows8 = jnp.where(sub == 0, mean, jnp.where(sub == 1, r_a, jnp.where(sub == 2, c_mean, c_norm)))

    for b in range(NC):
        wide = jnp.concatenate([rows8[:, b * TOK:(b + 1) * TOK]] * 16, axis=0).T
        at = slice(b * TOK, (b + 1) * TOK)
        a_norm = (att[at, :] - wide[:, 0:1]) * wide[:, 1:2]
        gate = g_s[at, :].astype(F32)
        incoming = gg[b].astype(F32)
        cot = incoming * gate
        gated_s[b] = (a_norm * gate).astype(BF16)
        dg_s[b] = (incoming * a_norm * slopes[at, :HD]).astype(BF16)
        d_att[at, :] = (wide[:, 1:2] * (cot - wide[:, 2:3] - a_norm * wide[:, 3:4])).astype(BF16)
    for k in range(1, NC):
        j = each_peer(k)
        remote(gated_s.at[j], gated_r.at[:, pl.ds(head, HD)], ex_s.at[0], ex_r.at[0], peer(j)).start()
        remote(dg_s.at[j], pg.at[:, pl.ds(head, HD)], ex_s.at[1], ex_r.at[1], peer(j)).start()
    gated_r[:, pl.ds(head, HD)] = gated_s[block]
    pg[:, pl.ds(head, HD)] = dg_s[block]

    dq_s[...] = jnp.zeros((SEQ, HD), F32)

    def backward(step, carry):
        kb = rem(block + 1 + step, NC)
        cols = pl.ds(pl.multiple_of(kb * TOK, TOK), TOK)
        d_kv[...] = jnp.zeros((TOK, 2 * HD), F32)

        def tile(qb, inner):
            rows = pl.ds(pl.multiple_of(qb * TOK, TOK), TOK)
            da = d_att[rows, :]
            slope = dot(da, v_s[cols, :], 1, 1)
            ds = (slope * d_t[tile_of(qb, kb)]).astype(BF16)
            dq_s[rows, :] += dot(ds, k_s[cols, :])
            d_kv[:, :HD] += dot(ds, q_s[rows, :], 0, 0)
            d_kv[:, HD:] += dot(w_t[tile_of(qb, kb)], da, 0, 0)
            return inner

        lax.fori_loop(kb, NC, tile, 0)
        both = (d_kv[...] * slopes[cols, 2 * HD:]).astype(BF16)
        dk_s[kb] = both[:, :HD]
        dv_s[kb] = both[:, HD:]

        @pl.when(kb != block)
        def _():
            remote(dk_s.at[kb], pg.at[:, pl.ds(2 * D + head, HD)], ex_s.at[2], ex_r.at[2], peer(kb)).start()
            remote(dv_s.at[kb], pg.at[:, pl.ds(3 * D + head, HD)], ex_s.at[3], ex_r.at[3], peer(kb)).start()

        return carry

    lax.fori_loop(0, NC, backward, 0)
    for b in range(NC):
        at = slice(b * TOK, (b + 1) * TOK)
        dqo_s[b] = (dq_s[at, :] * slopes[at, HD:2 * HD]).astype(BF16)
    for k in range(1, NC):
        j = each_peer(k)
        remote(dqo_s.at[j], pg.at[:, pl.ds(D + head, HD)], ex_s.at[4], ex_r.at[4], peer(j)).start()
    pg[:, pl.ds(D + head, HD)] = dqo_s[block]
    pg[:, pl.ds(2 * D + head, HD)] = dk_s[block]
    pg[:, pl.ds(3 * D + head, HD)] = dv_s[block]

    settle(gated_r.at[:, pl.ds(0, 3 * HD)], ex_r.at[0])
    mix[...] = (emb[...].astype(F32) + dot(gated_r[...], ow[...])).astype(BF16)

    @pl.when(away)
    def _():
        remote(mix, mixed, mx_s, mx_r, place(held)).start()

    @pl.when(jnp.logical_not(away))
    def _():
        mixed[...] = mix[...]

    for kind in range(1, 5):
        settle(pg.at[:, pl.ds(0, 3 * HD)], ex_r.at[kind])
    incoming = dot(pg[...], pw[...], 1, 1)
    norm = normed[...]
    embed_grad = r_x[...] * (
        incoming
        - jnp.mean(incoming, -1, keepdims=True)
        - norm * jnp.mean(incoming * norm, -1, keepdims=True)
    ) + og[...].astype(F32)
    embed_grad = embed_grad.astype(BF16)

    for step in range(ND // GROUP):
        group = rem(step + div(me, GROUP), ND // GROUP)
        first = pl.multiple_of(group * GROUP, GROUP)
        slots = iota((GROUP * CAP, TOK), 0) + group * (GROUP * CAP)
        sorted_rows = dot(one_hot(slots == slot_line.astype(jnp.int32)), embed_grad)
        halves = [sorted_rows[:, :256].reshape(GROUP, CAP, 256), sorted_rows[:, 256:].reshape(GROUP, CAP, 256)]
        out2[pl.ds(first, GROUP)] = jnp.concatenate(halves, axis=1).astype(BF16)

        def send(k, inner):
            target = first + rem(k + me, GROUP)

            @pl.when(target != me)
            def _():
                remote(out2.at[target], recv2.at[held], b_s, b_r, place(target)).start()

            @pl.when(target == me)
            def _():
                recv2[held] = out2[target]

            return inner

        lax.fori_loop(0, GROUP, send, 0)

    settle(vall.at[pl.ds(0, ND - 1)], ids_s)
    settle(out1.at[pl.ds(0, ND - 1)], a_s)
    settle(gg_send.at[pl.ds(0, 3)], gg_ss)
    for k in range(1, NC):
        settle(x_all.at[0], x_ss.at[k])
    settle(stats.at[pl.ds(0, 3)], st_s)
    for kind in range(5):
        settle(pg.at[:, pl.ds(0, 3 * HD)], ex_s.at[kind])

    @pl.when(away)
    def _():
        settle(og_in, og_s)
        settle(mix, mx_s)
        settle(mixed, mx_r)

    settle(out2.at[pl.ds(0, ND - 1)], b_s)
    settle(recv2.at[pl.ds(0, ND - 1)], b_r)


def scatter_kernel(wrow, recv2, out, rows):
    step = pl.program_id(0)

    @pl.when(step == 0)
    def _():
        for g in range(ND // GROUP):
            got = recv2[g * GROUP:(g + 1) * GROUP].astype(F32)
            rows[g * GROUP * CAP:(g + 1) * GROUP * CAP] = jnp.concatenate(
                [got[:, :CAP].reshape(GROUP * CAP, 256), got[:, CAP:].reshape(GROUP * CAP, 256)], axis=1
            ).astype(BF16)

    size = out.shape[0]
    wanted = wrow[...].astype(jnp.int32)
    out[...] = dot(one_hot((iota((size, SLOTS), 0) + step * size) == wanted), rows[...])


def shards(owner, row, lengths, table, proj_weight, out_weight, out_grad):
    vmem = pl.BlockSpec(memory_space=pltpu.VMEM)
    hbm = pl.BlockSpec(memory_space=pl.ANY)
    V = pltpu.VMEM
    DMA = pltpu.SemaphoreType.DMA
    mixed, recv2, wrow = pl.pallas_call(
        layer,
        out_shape=(
            jax.ShapeDtypeStruct((TOK, D), BF16),
            jax.ShapeDtypeStruct((ND, 2 * CAP, 256), BF16),
            jax.ShapeDtypeStruct((1, SLOTS), F32),
        ),
        in_specs=[vmem, vmem, pl.BlockSpec(memory_space=pltpu.SMEM), hbm, hbm, hbm, hbm],
        out_specs=(vmem, vmem, vmem),
        scratch_shapes=[
            V((ROWS, D), BF16), V((D, 4 * D), BF16), V((D, D), BF16), V((TOK, D), BF16), V((TOK, D), BF16),
            V((D, 4 * HD), BF16), V((1, 1, TOK), jnp.int32), V((ND, 1, TOK), jnp.int32),
            V((ND, 2 * CAP, 256), BF16), V((ND, 2 * CAP, 256), BF16), V((NC, TOK, D), BF16), V((TOK, D), BF16),
            V((TOK, D), F32), V((TOK, 1), F32),
            V((SEQ, HD), BF16), V((SEQ, HD), BF16), V((SEQ, HD), BF16), V((SEQ, HD), BF16), V((SEQ, 4 * HD), F32),
            V((NC, TOK, HD), BF16), V((NC, TOK, HD), BF16), V((SEQ, HD), F32), V((10, TOK, TOK), BF16), V((10, TOK, TOK), F32),
            V((SEQ, HD), BF16), V((SEQ, HD), F32),
            V((NC, TOK, HD), BF16), V((NC, TOK, HD), BF16), V((NC, TOK, HD), BF16), V((NC, TOK, HD), BF16),
            V((NC, TOK, HD), BF16),
            V((TOK, D), BF16), V((TOK, 4 * D), BF16), V((TOK, D), BF16), V((NC, 8, SEQ), F32),
            V((ND, 2 * CAP, 256), BF16), V((TOK, 2 * HD), F32),
            DMA((4,)), DMA, DMA, DMA, DMA, DMA, DMA, DMA, DMA, DMA((NC,)), DMA((NC,)), DMA, DMA,
            DMA((5,)), DMA((5,)), DMA, DMA, DMA, DMA,
        ],
        compiler_params=pltpu.CompilerParams(
            collective_id=0, has_side_effects=True, vmem_limit_bytes=52 * 1024 * 1024
        ),
    )(
        owner.reshape(1, TOK), row.reshape(1, TOK), lengths, table, proj_weight, out_weight,
        out_grad.reshape(TOK, D),
    )
    size = 256
    table_grad = pl.pallas_call(
        scatter_kernel,
        grid=(ROWS // size,),
        out_shape=jax.ShapeDtypeStruct((ROWS, D), F32),
        in_specs=[
            pl.BlockSpec((1, SLOTS), lambda i: (0, 0)),
            pl.BlockSpec((ND, 2 * CAP, 256), lambda i: (0, 0, 0)),
        ],
        out_specs=pl.BlockSpec((size, D), lambda i: (i, 0)),
        scratch_shapes=[V((SLOTS, D), BF16)],
        compiler_params=pltpu.CompilerParams(vmem_limit_bytes=32 * 1024 * 1024),
    )(wrow, recv2)
    return (mixed.reshape(1, TOK, D), table_grad)


def solution(mesh):
    placed = (
        P("user", "ctx", None),
        P("user", "ctx"),
        P("user"),
        P(("user", "ctx"), None),
        P(),
        P(),
        P("user", "ctx", None),
    )
    return jax.shard_map(
        shards,
        mesh=mesh,
        in_specs=placed,
        out_specs=(P("user", "ctx", None), P(("user", "ctx"), None)),
        check_vma=False,
    )
```

```python
import jax
import jax.numpy as jnp
from jax import lax
from jax.experimental import pallas as pl
from jax.experimental.pallas import tpu as pltpu
from jax.sharding import PartitionSpec as P

MESH = pl.DeviceIdType.MESH
F32 = jnp.float32
BF16 = jnp.bfloat16
NC = 4
ND = 128
TOK = 512
SEQ = 2048
D = 512
HD = 128
CAP = 8
ROWS = 2048
SLOTS = ND * CAP
GROUP = 32
EPSILON = 1e-05
SCALE = HD ** (-0.5)
QT = 256
UNROLL = 16


def div(a, b):
    return lax.div(a, jnp.int32(b))


def rem(a, b):
    return lax.rem(a, jnp.int32(b))


def number_at(x, y, z, core):
    return ((rem(x + y + z, 4) * 4 + z) * 2 + core) * 4 + x


def coords(number):
    x, core, z = rem(number, 4), rem(div(number, 4), 2), rem(div(number, 8), 4)
    return x, rem(div(number, 32) + 8 - x - z, 4), z, core


def worker(number):
    x, y, z, core = coords(number)
    return number_at(x + core * (y - x), y + core * (rem(x + y, 4) - y), z, core)


def holder(number):
    x, y, z, core = coords(number)
    return number_at(x + core * (rem(y + 4 - x, 4) - x), y + core * (x - y), z, core)


def place(number):
    x, y, z, core = coords(number)
    return ((y * 4 + z) * 2 + core, x)


def iota(shape, axis):
    return lax.broadcasted_iota(jnp.int32, shape, axis)


def to_column(line):
    n = line.shape[1]
    eye = iota((n, n), 0) == iota((n, n), 1)
    return jnp.sum(jnp.where(eye, line, 0.0), axis=1, keepdims=True)


def to_line(column):
    n = column.shape[0]
    eye = iota((n, n), 0) == iota((n, n), 1)
    return jnp.sum(jnp.where(eye, column, 0.0), axis=0, keepdims=True)


def one_hot(match):
    return jnp.where(match, 1.0, 0.0).astype(BF16)


def dot(a, b, ca=1, cb=0):
    return lax.dot_general(a, b, (((ca,), (cb,)), ((), ())), preferred_element_type=F32)


def others(act, width=UNROLL):
    whole = (ND - 1) // width

    def some(step, carry):
        for k in range(width):
            act(step * width + (k + 1))
        return carry

    lax.fori_loop(0, whole, some, 0)
    for k in range(whole * width + 1, ND):
        act(jnp.int32(k))


def members(act, width=UNROLL):
    def some(step, carry):
        for k in range(width):
            act(step * width + k)
        return carry

    lax.fori_loop(0, GROUP // width, some, 0)


def remote(src, dst, send, recv, target):
    return pltpu.make_async_remote_copy(
        src_ref=src, dst_ref=dst, send_sem=send, recv_sem=recv, device_id=target, device_id_type=MESH
    )


def tile_of(q, k):
    return div(q * (q + 1), 2) + k


def settle(view, sem):
    pltpu.make_async_copy(view, view, sem).wait()


def silu_parts(values):
    half = values * 0.5
    t = jnp.tanh(half)
    turned = half * t
    return half + turned, (0.5 + 0.5 * t) * (1.0 + (half - turned))


def layer(
    owner, row, length, table_h, pw_h, ow_h, og_h,
    mixed, recv2, wrow,
    table, pw, ow, og, og_in, og_mid, vbuf, vall, out1, recv1, emb, normed, r_x, slopes, gate_s, gg,
    out_q, out_k, out_v, out_c, out_an, out_dk, out_dv, out_dq, q_s, k_s, v_s, c_s, an_s, dqkv,
    att, w_t, d_t, d_att, d_att_t, q_t, dq_acc, d_kv, e_acc, mix, stats, out2,
    load, ids_s, ids_r, og_s, og_r, a_s, a_r, st_s, st_r, ex_s, ex_r, mx_s, mx_r, b_s, b_r,
):
    user, ctx = lax.axis_index("user"), lax.axis_index("ctx")
    core, z_at, y_at = rem(user, 2), rem(div(user, 2), 4), div(user, 8)
    me = number_at(ctx, y_at, z_at, core)
    held = holder(me)
    relay = number_at(ctx, y_at + core * (rem(ctx + y_at, 4) - y_at), z_at, core)
    beyond = number_at(ctx + core * (rem(y_at + 4 - ctx, 4) - ctx), y_at, z_at, core)
    block = rem(held, NC)
    away = held != me

    def peer(j):
        other = (rem(j + ctx, 4) * 4 + z_at) * 2 + 1
        return (user + core * (other - user), j + core * (ctx - j))

    def each_peer(k):
        return rem(block + k, NC)

    barrier = pltpu.get_barrier_semaphore()

    def greet(k):
        pl.semaphore_signal(barrier, inc=1, device_id=place(rem(me + k, ND)), device_id_type=MESH)

    others(greet)

    head = pl.multiple_of(block * HD, HD)
    loads = [
        pltpu.make_async_copy(og_h, og_in, load.at[0]),
        pltpu.make_async_copy(table_h, table, load.at[1]),
        pltpu.make_async_copy(ow_h, ow, load.at[2]),
        pltpu.make_async_copy(pw_h, pw, load.at[3]),
    ]
    for copy in loads:
        copy.start()

    places = ctx * TOK + iota((1, TOK), 1)
    valid = places < length[0]
    own_x, own_y = jnp.bitwise_and(owner[...], 3), lax.shift_right_logical(owner[...], 5)
    own_z = jnp.bitwise_and(lax.shift_right_logical(owner[...], 3), 3)
    own_w = jnp.bitwise_and(own_x + own_y + own_z, 3)
    own = jnp.where(valid, jnp.bitwise_and(owner[...], 31) + own_w * 32, -1)
    match = iota((ND, TOK), 0) == own
    before = one_hot(iota((TOK, TOK), 0) < iota((TOK, TOK), 1))
    rank = dot(one_hot(match), before)
    slot = jnp.sum(jnp.where(match, rank, 0.0), axis=0, keepdims=True).astype(jnp.int32)
    packed = jnp.where(valid, (own * CAP + slot) * ROWS + row[...], -1)
    vbuf[0] = packed
    vall[me] = packed

    pl.semaphore_wait(barrier, ND - 1)

    def tell(k):
        remote(vbuf.at[0], vall.at[me], ids_s, ids_r, place(rem(me + k, ND))).start()

    loads[0].wait()

    @pl.when(relay != me)
    def _():
        remote(og_in, og_mid, og_s.at[0], og_r.at[0], place(relay)).start()

    @pl.when(relay == me)
    def _():
        og_mid[...] = og_in[...]

    others(tell)
    settle(vall.at[pl.ds(0, ND - 1)], ids_r)

    @pl.when(relay != me)
    def _():
        settle(og_mid, og_r.at[0])

    @pl.when(beyond != me)
    def _():
        remote(og_mid, og, og_s.at[1], og_r.at[1], place(beyond)).start()

    loads[1].wait()

    def answer(step, carry):
        group = rem(step + div(me, GROUP), ND // GROUP)
        first = pl.multiple_of(group * GROUP, GROUP)
        asked = vall[pl.ds(first, GROUP)]
        mine = (lax.shift_right_arithmetic(asked, 11) - me * CAP) == iota((GROUP, CAP, 1), 1)
        wanted = jnp.where(mine, (jnp.bitwise_and(asked, ROWS - 1) + 1).astype(F32), 0.0)
        wanted = (jnp.sum(wanted, axis=2, keepdims=True) - 1.0).reshape(GROUP * CAP, 1)
        wrow[:, pl.ds(pl.multiple_of(group * GROUP * CAP, GROUP * CAP), GROUP * CAP)] = to_line(wanted)
        found = dot(one_hot(iota((GROUP * CAP, ROWS), 1) == wanted.astype(jnp.int32)), table[...])
        halves = [found[:, :256].reshape(GROUP, CAP, 256), found[:, 256:].reshape(GROUP, CAP, 256)]
        out1[pl.ds(first, GROUP)] = jnp.concatenate(halves, axis=1).astype(BF16)

        def send(k):
            source = first + rem(k + me, GROUP)
            target = worker(source)

            @pl.when(target != me)
            def _():
                remote(out1.at[source], recv1.at[me], a_s, a_r, place(target)).start()

            @pl.when(target == me)
            def _():
                recv1[me] = out1[source]

        members(send)
        return carry

    lax.fori_loop(0, ND // GROUP, answer, 0)

    slot_line = lax.shift_right_arithmetic(vall[held], 11).astype(F32)
    slot_col = to_column(slot_line)
    loads[2].wait()
    loads[3].wait()

    @pl.when(beyond != me)
    def _():
        settle(og, og_r.at[1])

    @pl.when(beyond == me)
    def _():
        og[...] = og_mid[...]

    masked = jnp.where(slot_col >= 0.0, og[...], jnp.zeros((TOK, D), BF16))
    og[...] = masked
    gg[...] = dot(masked, ow[...], 1, 1)

    settle(recv1.at[pl.ds(0, ND - 1)], a_r)
    embed = jnp.zeros((TOK, D), F32)
    for g in range(ND // GROUP):
        got = recv1[g * GROUP:(g + 1) * GROUP].astype(F32)
        rows = jnp.concatenate(
            [got[:, :CAP].reshape(GROUP * CAP, 256), got[:, CAP:].reshape(GROUP * CAP, 256)], axis=1
        ).astype(BF16)
        lanes = iota((TOK, GROUP * CAP), 1) + g * GROUP * CAP
        embed = embed + dot(one_hot(lanes == slot_col.astype(jnp.int32)), rows)
    emb[...] = embed.astype(BF16)
    center = jnp.mean(embed, -1, keepdims=True)
    deviation = embed - center
    inverse = lax.rsqrt(jnp.mean(deviation * deviation, -1, keepdims=True) + EPSILON)
    norm = deviation * inverse
    normed[...] = norm
    r_x[...] = inverse
    norm_low = norm.astype(BF16)

    def spread(low, outbox, inbox, kind):
        for j in range(NC):
            outbox[j] = low[:, j * HD:(j + 1) * HD]
        for k in range(1, NC):
            j = each_peer(k)
            remote(outbox.at[j], inbox.at[block], ex_s.at[kind], ex_r.at[kind], peer(j)).start()
        inbox[block] = outbox[block]

    for kind, (outbox, inbox) in enumerate(((out_q, q_s), (out_k, k_s), (out_v, v_s))):
        part = slice((kind + 1) * D, (kind + 2) * D)
        silu, slope = silu_parts(dot(norm_low, pw[:, part]))
        slopes[:, part] = slope
        spread(silu.astype(BF16), outbox, inbox, kind)

    silu, slope = silu_parts(dot(norm_low, pw[:, :D]))
    slopes[:, :D] = slope
    gate = silu.astype(BF16)
    gate_s[...] = gate
    spread((gg[...] * gate.astype(F32)).astype(BF16), out_c, c_s, 3)
    for kind, inbox in enumerate((q_s, k_s, v_s)):
        settle(inbox.at[pl.ds(0, 3)], ex_r.at[kind])

    def forward(qb, carry):
        big, half = div(qb, 2), pl.ds(pl.multiple_of(rem(qb, 2) * QT, QT), QT)
        query = q_s[big, half, :]

        def tile(kb, total, diagonal):
            half_score = dot(query, k_s[kb], 1, 1) * (0.5 * SCALE)
            t = jnp.tanh(half_score)
            turned = half_score * t
            weights = half_score + turned
            slope = (1.0 + t) * ((1.0 + half_score) - turned) * (0.5 * SCALE)
            if diagonal:
                allowed = (iota((QT, TOK), 1) - iota((QT, TOK), 0)) <= (qb * QT - kb * TOK)
                weights = jnp.where(allowed, weights, 0.0)
                slope = jnp.where(allowed, slope, 0.0)
            weights = weights.astype(BF16)
            w_t[tile_of(big, kb), half, :] = weights
            d_t[tile_of(big, kb), half, :] = slope
            return total + dot(weights, v_s[kb])

        total = lax.fori_loop(0, big, lambda kb, total: tile(kb, total, False), jnp.zeros((QT, HD), F32))
        att[big, half, :] = tile(big, total, True)
        return carry

    lax.fori_loop(0, SEQ // QT, forward, 0)

    settle(c_s.at[pl.ds(0, 3)], ex_r.at[3])
    for b in range(NC):
        total = att[b]
        cot = c_s[b].astype(F32)
        mean = jnp.mean(total, -1, keepdims=True)
        off = total - mean
        spread_sum = jnp.sum(off * off, -1, keepdims=True)
        c_sum = jnp.sum(cot, -1, keepdims=True)
        c_off = jnp.sum(cot * off, -1, keepdims=True)
        lane = iota((TOK, HD), 1)
        table4 = jnp.where(lane == 0, mean, jnp.where(lane == 1, spread_sum, jnp.where(lane == 2, c_sum, c_off)))
        stats[block, :, b * TOK:(b + 1) * TOK] = table4.T[:8]
    for k in range(1, NC):
        remote(stats.at[block], stats.at[block], st_s, st_r, peer(each_peer(k))).start()
    for b in range(NC):
        q_t[b] = q_s[b].astype(F32).T.astype(BF16)
    settle(stats.at[pl.ds(0, 3)], st_r)

    means = [stats[h, 0:1, :] for h in range(NC)]
    mean = (means[0] + means[1] + means[2] + means[3]) * (1.0 / NC)
    spread_sum = 0.0
    c_sum = 0.0
    c_off = 0.0
    for h in range(NC):
        gap = means[h] - mean
        spread_sum = spread_sum + stats[h, 1:2, :] + HD * gap * gap
        c_sum = c_sum + stats[h, 2:3, :]
        c_off = c_off + stats[h, 3:4, :] + stats[h, 2:3, :] * gap
    r_a = lax.rsqrt(spread_sum * (1.0 / D) + EPSILON)
    c_mean = c_sum * (1.0 / D)
    c_norm = r_a * c_off * (1.0 / D)
    sub = iota((8, SEQ), 0)
    rows8 = jnp.where(sub == 0, mean, jnp.where(sub == 1, r_a, jnp.where(sub == 2, c_mean, c_norm)))

    for b in range(NC):
        wide = jnp.concatenate([rows8[:, b * TOK:(b + 1) * TOK]] * 16, axis=0).T
        a_norm = (att[b] - wide[:, 0:1]) * wide[:, 1:2]
        out_an[b] = a_norm.astype(BF16)
        grad = wide[:, 1:2] * (c_s[b].astype(F32) - wide[:, 2:3] - a_norm * wide[:, 3:4])
        d_att[b] = grad.astype(BF16)
        d_att_t[b] = grad.T.astype(BF16)
    for k in range(1, NC):
        j = each_peer(k)
        remote(out_an.at[j], an_s.at[:, pl.ds(head, HD)], ex_s.at[4], ex_r.at[4], peer(j)).start()
    an_s[:, pl.ds(head, HD)] = out_an[block]

    dq_acc[...] = jnp.zeros((NC, TOK, HD), F32)

    def backward(step, carry):
        kb = rem(block + 1 + step, NC)
        d_kv[...] = jnp.zeros((2, HD, TOK), F32)

        def tile(qb, inner):
            slope = dot(d_att[qb], v_s[kb], 1, 1)
            ds = (slope * d_t[tile_of(qb, kb)]).astype(BF16)
            dq_acc[qb] += dot(ds, k_s[kb])
            d_kv[0] += dot(q_t[qb], ds)
            d_kv[1] += dot(d_att_t[qb], w_t[tile_of(qb, kb)])
            return inner

        lax.fori_loop(kb, NC, tile, 0)
        out_dk[kb] = d_kv[0].T.astype(BF16)
        out_dv[kb] = d_kv[1].T.astype(BF16)

        @pl.when(kb != block)
        def _():
            remote(out_dk.at[kb], dqkv.at[:, pl.ds(D + head, HD)], ex_s.at[5], ex_r.at[5], peer(kb)).start()
            remote(out_dv.at[kb], dqkv.at[:, pl.ds(2 * D + head, HD)], ex_s.at[6], ex_r.at[6], peer(kb)).start()

        return carry

    lax.fori_loop(0, 2, backward, 0)

    settle(an_s.at[:, pl.ds(0, 3 * HD)], ex_r.at[4])
    a_norm = an_s[...].astype(F32)
    gated = (a_norm * gate_s[...].astype(F32)).astype(BF16)
    mix[...] = (emb[...].astype(F32) + dot(gated, ow[...])).astype(BF16)

    @pl.when(away)
    def _():
        remote(mix, mixed, mx_s, mx_r, place(held)).start()

    @pl.when(jnp.logical_not(away))
    def _():
        mixed[...] = mix[...]

    e_acc[...] = dot((gg[...] * a_norm * slopes[:, :D]).astype(BF16), pw[:, :D], 1, 1)

    lax.fori_loop(2, NC, backward, 0)
    for b in range(NC):
        out_dq[b] = dq_acc[b].astype(BF16)
    for k in range(1, NC):
        j = each_peer(k)
        remote(out_dq.at[j], dqkv.at[:, pl.ds(head, HD)], ex_s.at[7], ex_r.at[7], peer(j)).start()
    dqkv[:, pl.ds(head, HD)] = out_dq[block]
    dqkv[:, pl.ds(D + head, HD)] = out_dk[block]
    dqkv[:, pl.ds(2 * D + head, HD)] = out_dv[block]

    incoming = e_acc[...]
    for kind, part in ((5, 1), (6, 2), (7, 0)):
        settle(an_s.at[:, pl.ds(0, 3 * HD)], ex_r.at[kind])
        grad = dqkv[:, part * D:(part + 1) * D].astype(F32) * slopes[:, (part + 1) * D:(part + 2) * D]
        incoming = incoming + dot(grad.astype(BF16), pw[:, (part + 1) * D:(part + 2) * D], 1, 1)
    norm = normed[...]
    embed_grad = r_x[...] * (
        incoming
        - jnp.mean(incoming, -1, keepdims=True)
        - norm * jnp.mean(incoming * norm, -1, keepdims=True)
    ) + og[...].astype(F32)
    embed_grad = embed_grad.astype(BF16)

    for step in range(ND // GROUP):
        group = rem(step + div(me, GROUP), ND // GROUP)
        first = pl.multiple_of(group * GROUP, GROUP)
        slots = iota((GROUP * CAP, TOK), 0) + group * (GROUP * CAP)
        sorted_rows = dot(one_hot(slots == slot_line.astype(jnp.int32)), embed_grad)
        halves = [sorted_rows[:, :256].reshape(GROUP, CAP, 256), sorted_rows[:, 256:].reshape(GROUP, CAP, 256)]
        out2[pl.ds(first, GROUP)] = jnp.concatenate(halves, axis=1).astype(BF16)

        def send(k):
            target = first + rem(k + me, GROUP)

            @pl.when(target != me)
            def _():
                remote(out2.at[target], recv2.at[held], b_s, b_r, place(target)).start()

            @pl.when(target == me)
            def _():
                recv2[held] = out2[target]

        members(send)

    settle(vall.at[pl.ds(0, ND - 1)], ids_s)
    settle(out1.at[pl.ds(0, ND - 1)], a_s)
    settle(stats.at[pl.ds(0, 3)], st_s)
    for kind in range(8):
        settle(out_q.at[pl.ds(0, 3)], ex_s.at[kind])

    @pl.when(relay != me)
    def _():
        settle(og_in, og_s.at[0])

    @pl.when(beyond != me)
    def _():
        settle(og_mid, og_s.at[1])

    @pl.when(away)
    def _():
        settle(mix, mx_s)
        settle(mixed, mx_r)

    settle(out2.at[pl.ds(0, ND - 1)], b_s)
    settle(recv2.at[pl.ds(0, ND - 1)], b_r)


def scatter_kernel(wrow, recv2, mix, out, mixed, rows):
    step = pl.program_id(0)

    @pl.when(step == 0)
    def _():
        for g in range(ND // GROUP):
            got = recv2[g * GROUP:(g + 1) * GROUP].astype(F32)
            rows[g * GROUP * CAP:(g + 1) * GROUP * CAP] = jnp.concatenate(
                [got[:, :CAP].reshape(GROUP * CAP, 256), got[:, CAP:].reshape(GROUP * CAP, 256)], axis=1
            ).astype(BF16)

    mixed[...] = mix[...]
    size = out.shape[0]
    wanted = wrow[...].astype(jnp.int32) - step * size
    for part in range(size // 256):
        at = slice(part * 256, (part + 1) * 256)
        out[at, :] = dot(one_hot(iota((256, SLOTS), 0) + part * 256 == wanted), rows[...])


def shards(owner, row, lengths, table, proj_weight, out_weight, out_grad):
    vmem = pl.BlockSpec(memory_space=pltpu.VMEM)
    hbm = pl.BlockSpec(memory_space=pltpu.HBM)
    V = pltpu.VMEM
    DMA = pltpu.SemaphoreType.DMA
    mixed, recv2, wrow = pl.pallas_call(
        layer,
        out_shape=(
            jax.ShapeDtypeStruct((TOK, D), BF16),
            jax.ShapeDtypeStruct((ND, 2 * CAP, 256), BF16),
            jax.ShapeDtypeStruct((1, SLOTS), F32),
        ),
        in_specs=[vmem, vmem, pl.BlockSpec(memory_space=pltpu.SMEM), hbm, hbm, hbm, hbm],
        out_specs=(vmem, vmem, vmem),
        scratch_shapes=[
            V((ROWS, D), BF16), V((D, 4 * D), BF16), V((D, D), BF16), V((TOK, D), BF16), V((TOK, D), BF16), V((TOK, D), BF16),
            V((1, 1, TOK), jnp.int32), V((ND, 1, TOK), jnp.int32),
            V((ND, 2 * CAP, 256), BF16), V((ND, 2 * CAP, 256), BF16), V((TOK, D), BF16),
            V((TOK, D), F32), V((TOK, 1), F32), V((TOK, 4 * D), F32), V((TOK, D), BF16), V((TOK, D), F32),
        ] + [V((NC, TOK, HD), BF16)] * 12 + [
            V((TOK, D), BF16), V((TOK, 3 * D), BF16),
            V((NC, TOK, HD), F32), V((10, TOK, TOK), BF16), V((10, TOK, TOK), F32),
            V((NC, TOK, HD), BF16), V((NC, HD, TOK), BF16), V((NC, HD, TOK), BF16),
            V((NC, TOK, HD), F32), V((2, HD, TOK), F32), V((TOK, D), F32), V((TOK, D), BF16), V((NC, 8, SEQ), F32),
            V((ND, 2 * CAP, 256), BF16),
            DMA((4,)), DMA, DMA, DMA((2,)), DMA((2,)), DMA, DMA, DMA, DMA, DMA((8,)), DMA((8,)), DMA, DMA, DMA, DMA,
        ],
        compiler_params=pltpu.CompilerParams(
            collective_id=0, has_side_effects=True, vmem_limit_bytes=52 * 1024 * 1024
        ),
    )(
        owner.reshape(1, TOK), row.reshape(1, TOK), lengths, table, proj_weight, out_weight,
        out_grad.reshape(TOK, D),
    )
    steps = 4
    table_grad, mixed = pl.pallas_call(
        scatter_kernel,
        grid=(steps,),
        out_shape=(jax.ShapeDtypeStruct((ROWS, D), F32), jax.ShapeDtypeStruct((TOK, D), BF16)),
        in_specs=[vmem, vmem, pl.BlockSpec((TOK // steps, D), lambda i: (i, 0))],
        out_specs=(
            pl.BlockSpec((ROWS // steps, D), lambda i: (i, 0)),
            pl.BlockSpec((TOK // steps, D), lambda i: (i, 0)),
        ),
        scratch_shapes=[V((SLOTS, D), BF16)],
        compiler_params=pltpu.CompilerParams(vmem_limit_bytes=32 * 1024 * 1024),
    )(wrow, recv2, mixed)
    return (mixed.reshape(1, TOK, D), table_grad)


def solution(mesh):
    placed = (
        P("user", "ctx", None),
        P("user", "ctx"),
        P("user"),
        P(("user", "ctx"), None),
        P(),
        P(),
        P("user", "ctx", None),
    )
    return jax.shard_map(
        shards,
        mesh=mesh,
        in_specs=placed,
        out_specs=(P("user", "ctx", None), P(("user", "ctx"), None)),
        check_vma=False,
    )
```

```python
import jax
import jax.numpy as jnp
from jax import lax
from jax.experimental import pallas as pl
from jax.experimental.pallas import tpu as pltpu
from jax.sharding import PartitionSpec as P

MESH = pl.DeviceIdType.MESH
F32 = jnp.float32
BF16 = jnp.bfloat16
NC = 4
ND = 128
TOK = 512
SEQ = 2048
D = 512
HD = 128
CAP = 8
ROWS = 2048
SLOTS = ND * CAP
GROUP = 32
EPSILON = 1e-05
SCALE = HD ** (-0.5)
QT = 256


def div(a, b):
    return lax.div(a, jnp.int32(b))


def rem(a, b):
    return lax.rem(a, jnp.int32(b))


SETS = sorted(((dy, dz) for dy in range(4) for dz in range(4)), key=lambda d: -((0, 1, 2, 1)[d[0]] + (0, 1, 2, 1)[d[1]]))
HERE = SETS.index((0, 0)) * 8


def opposite_set(k):
    return SETS.index(((4 - SETS[k][0]) % 4, (4 - SETS[k][1]) % 4))


def opposite_member(k):
    return k // 4 * 4 + (4 - k % 4) % 4


def opposite(k):
    return opposite_set(k // 8) * 8 + opposite_member(k % 8)


def order_of(first):
    far = (0, 1, 2, 1)
    return sorted(
        range(first, first + GROUP),
        key=lambda k: -(far[SETS[k // 8][0]] + far[SETS[k // 8][1]] + far[k % 4]),
    )


def iota(shape, axis):
    return lax.broadcasted_iota(jnp.int32, shape, axis)


def to_column(line):
    n = line.shape[1]
    eye = iota((n, n), 0) == iota((n, n), 1)
    return jnp.sum(jnp.where(eye, line, 0.0), axis=1, keepdims=True)


def to_line(column):
    n = column.shape[0]
    eye = iota((n, n), 0) == iota((n, n), 1)
    return jnp.sum(jnp.where(eye, column, 0.0), axis=0, keepdims=True)


def one_hot(match):
    return jnp.where(match, 1.0, 0.0).astype(BF16)


def dot(a, b, ca=1, cb=0):
    return lax.dot_general(a, b, (((ca,), (cb,)), ((), ())), preferred_element_type=F32)


def remote(src, dst, send, recv, target):
    return pltpu.make_async_remote_copy(
        src_ref=src, dst_ref=dst, send_sem=send, recv_sem=recv, device_id=target, device_id_type=MESH
    )


def tile_of(q, k):
    return div(q * (q + 1), 2) + k


def settle(view, sem):
    pltpu.make_async_copy(view, view, sem).wait()


def silu_parts(values):
    half = values * 0.5
    t = jnp.tanh(half)
    turned = half * t
    return half + turned, (0.5 + 0.5 * t) * (1.0 + (half - turned))


def layer(
    owner, row, length, table_h, pw_h, ow_h, og_h,
    mixed, recv2, wrow,
    table, pw, ow, og, og_in, og_mid, v_out, v_held, ask_out, ask_mid, ask_in, out1, recv1, emb, normed, r_x, slopes, gate_s, gg,
    out_q, out_k, out_v, out_off, out_da, out_dk, out_dv, out_dq, q_s, k_s, v_s, da_s, off_s, dqkv, out_m, m_s,
    an_s, att, w_t, d_t, da_t, q_t, dq_acc, d_kv, e_acc, mix, out2,
    load, ids_s, ids_r, og_s, og_r, a_s, a_r, ex_s, ex_r, mx_s, mx_r, b_s, b_r,
):
    user, ctx = lax.axis_index("user"), lax.axis_index("ctx")
    core, z_at, y_at = rem(user, 2), rem(div(user, 2), 4), div(user, 8)

    def device(x, y, z=z_at, c=core):
        return ((y * 4 + z) * 2 + c, x)

    xs = [rem(ctx + d, 4) for d in range(4)]
    ys = [rem(y_at + d, 4) for d in range(4)]
    zs = [rem(z_at + d, 4) for d in range(4)]
    cores = [core, 1 - core]

    def place(k):
        dy, dz = SETS[k // 8]
        return device(xs[k % 4], ys[dy], zs[dz], cores[k % 8 // 4])

    work_x, work_y = ctx + core * (y_at - ctx), y_at + core * (rem(ctx + y_at, 4) - y_at)
    back = rem(y_at + 4 - ctx, 4)
    held_x, held_y = ctx + core * (back - ctx), y_at + core * (ctx - y_at)
    block = held_x
    away = jnp.logical_or(work_x != ctx, work_y != y_at)
    relay_away, beyond_away = work_y != y_at, held_x != ctx

    def peer(j):
        other = (rem(j + ctx, 4) * 4 + z_at) * 2 + 1
        return (user + core * (other - user), j + core * (ctx - j))

    def each_peer(k):
        return rem(block + k, NC)

    barrier = pltpu.get_barrier_semaphore()

    for k in range(ND):
        if k != HERE:
            pl.semaphore_signal(barrier, inc=1, device_id=place(k), device_id_type=MESH)

    head = pl.multiple_of(block * HD, HD)
    loads = [
        pltpu.make_async_copy(og_h, og_in, load.at[0]),
        pltpu.make_async_copy(table_h, table, load.at[1]),
        pltpu.make_async_copy(ow_h, ow, load.at[2]),
        pltpu.make_async_copy(pw_h, pw, load.at[3]),
    ]
    for copy in loads:
        copy.start()

    places = ctx * TOK + iota((1, TOK), 1)
    valid = places < length[0]
    who = owner[...]
    far_x = jnp.bitwise_and(who + (4 - work_x), 3)
    far_core = jnp.bitwise_and(lax.shift_right_logical(who, 2) + core, 1)
    far_z = jnp.bitwise_and(lax.shift_right_logical(who, 3) + (4 - z_at), 3)
    far_y = jnp.bitwise_and(lax.shift_right_logical(who, 5) + (4 - work_y), 3)
    far_set = jnp.zeros((1, TOK), jnp.int32)
    for number, (dy, dz) in enumerate(SETS):
        far_set = jnp.where(far_y * 4 + far_z == dy * 4 + dz, number, far_set)
    own = jnp.where(valid, far_set * 8 + far_core * 4 + far_x, -1)
    match = iota((ND, TOK), 0) == own
    before = one_hot(iota((TOK, TOK), 0) < iota((TOK, TOK), 1))
    rank = dot(one_hot(match), before)
    slot = jnp.sum(jnp.where(match, rank, 0.0), axis=0, keepdims=True).astype(jnp.int32)
    slot_own = jnp.where(valid, own * CAP + slot, -1)
    v_out[0] = slot_own

    lane_own = jnp.where(valid, lax.shift_right_arithmetic(own, 3) * CAP + slot, -1)
    lanes_hot = one_hot(iota((TOK, ND), 1) == to_column(lane_own.astype(F32)).astype(jnp.int32))
    sub16 = iota((16, TOK), 0)
    digits = jnp.where(sub16 < 8, lax.shift_right_arithmetic(row[...] + 1, 6), jnp.bitwise_and(row[...] + 1, 63))
    digits = jnp.where(jnp.bitwise_and(sub16, 7) == far_core * 4 + far_x, digits, 0).astype(F32).astype(BF16)
    lines = dot(digits, lanes_hot)
    lines = lines[:8] * 64.0 + lines[8:]
    for member in range(8):
        ask_out[member] = lines[member:member + 1]

    pl.semaphore_wait(barrier, ND - 1)

    for member in range(8):
        line_x, line_core = rem(work_x + member % 4, 4), rem(core + member // 4, 2)
        here = jnp.logical_and(jnp.logical_and(line_x == ctx, line_core == core), work_y == y_at)

        @pl.when(jnp.logical_not(here))
        def _():
            target = device(line_x, work_y, z_at, line_core)
            line = ask_mid.at[opposite_member(member)]
            remote(ask_out.at[member], line, ids_s.at[0], ids_r.at[0], target).start()

        @pl.when(here)
        def _():
            ask_mid[opposite_member(member)] = ask_out[member]

    @pl.when(away)
    def _():
        remote(v_out, v_held, ids_s.at[2], ids_r.at[2], device(work_x, work_y)).start()

    @pl.when(jnp.logical_not(away))
    def _():
        v_held[0] = slot_own

    loads[0].wait()

    @pl.when(relay_away)
    def _():
        remote(og_in, og_mid, og_s.at[0], og_r.at[0], device(ctx, work_y)).start()

    @pl.when(jnp.logical_not(relay_away))
    def _():
        og_mid[...] = og_in[...]

    @pl.when(relay_away)
    def _():
        settle(ask_mid, ids_r.at[0])

    @pl.when(jnp.logical_not(relay_away))
    def _():
        settle(ask_mid.at[pl.ds(0, 7)], ids_r.at[0])

    for number in range(16):
        if number * 8 != HERE:
            lines = ask_in.at[pl.ds(opposite_set(number) * 8, 8)]
            remote(ask_mid, lines, ids_s.at[1], ids_r.at[1], place(number * 8)).start()
    ask_in[HERE:HERE + 8] = ask_mid[...]
    settle(ask_in.at[pl.ds(0, 120)], ids_r.at[1])
    loads[1].wait()

    for first in range(0, ND, GROUP):
        wanted = []
        for number in range(first // 8, (first + GROUP) // 8):
            mine = iota((1, CAP, ND), 2) == iota((1, CAP, ND), 1) + opposite_set(number) * CAP
            lines = jnp.where(mine, ask_in[number * 8:number * 8 + 8], 0.0)
            wanted.append(jnp.sum(lines, axis=2, keepdims=True).reshape(8 * CAP, 1))
        wanted = jnp.concatenate(wanted, axis=0) - 1.0
        wrow[:, first * CAP:(first + GROUP) * CAP] = to_line(wanted)
        found = dot(one_hot(iota((GROUP * CAP, ROWS), 1) == wanted.astype(jnp.int32)), table[...])
        halves = [found[:, :256].reshape(GROUP, CAP, 256), found[:, 256:].reshape(GROUP, CAP, 256)]
        out1[first:first + GROUP] = jnp.concatenate(halves, axis=1).astype(BF16)
        for k in order_of(first):
            if k != HERE:
                remote(out1.at[k], recv1.at[opposite(k)], a_s, a_r, place(k)).start()
    recv1[HERE] = out1[HERE]

    @pl.when(away)
    def _():
        settle(v_held, ids_r.at[2])

    slot_line = v_held[0].astype(F32)
    slot_col = to_column(slot_line)
    loads[2].wait()
    loads[3].wait()

    settle(recv1.at[pl.ds(0, ND - 1)], a_r)
    embed = jnp.zeros((TOK, D), F32)
    for g in range(ND // GROUP):
        got = recv1[g * GROUP:(g + 1) * GROUP].astype(F32)
        rows = jnp.concatenate(
            [got[:, :CAP].reshape(GROUP * CAP, 256), got[:, CAP:].reshape(GROUP * CAP, 256)], axis=1
        ).astype(BF16)
        lanes = iota((TOK, GROUP * CAP), 1) + g * GROUP * CAP
        embed = embed + dot(one_hot(lanes == slot_col.astype(jnp.int32)), rows)
    emb[...] = embed.astype(BF16)
    center = jnp.mean(embed, -1, keepdims=True)
    deviation = embed - center
    inverse = lax.rsqrt(jnp.mean(deviation * deviation, -1, keepdims=True) + EPSILON)
    norm = deviation * inverse
    normed[...] = norm
    r_x[...] = inverse
    norm_low = norm.astype(BF16)

    for kind, (outbox, inbox) in enumerate(((out_q, q_s), (out_k, k_s), (out_v, v_s))):
        part = slice((kind + 1) * D, (kind + 2) * D)
        silu, slope = silu_parts(dot(norm_low, pw[:, part]))
        slopes[:, part] = slope
        low = silu.astype(BF16)
        for j in range(NC):
            outbox[j] = low[:, j * HD:(j + 1) * HD]
        inbox[block] = outbox[block]
    for k in (1, 3, 2):
        j = each_peer(k)
        for outbox, inbox in ((out_q, q_s), (out_k, k_s), (out_v, v_s)):
            remote(outbox.at[j], inbox.at[block], ex_s.at[k - 1], ex_r.at[k - 1], peer(j)).start()

    silu, slope = silu_parts(dot(norm_low, pw[:, :D]))
    slopes[:, :D] = slope
    gate_s[...] = silu.astype(BF16)

    def tile(qb, kb, diagonal):
        for part in range(TOK // QT):
            half = slice(part * QT, (part + 1) * QT)
            half_score = dot(q_s[qb, half, :], k_s[kb], 1, 1) * (0.5 * SCALE)
            t = jnp.tanh(half_score)
            turned = half_score * t
            weights = half_score + turned
            slope = (1.0 + t) * ((1.0 + half_score) - turned) * (0.5 * SCALE)
            if diagonal:
                allowed = (iota((QT, TOK), 1) - iota((QT, TOK), 0)) <= part * QT
                weights = jnp.where(allowed, weights, 0.0)
                slope = jnp.where(allowed, slope, 0.0)
            weights = weights.astype(BF16)
            w_t[tile_of(qb, kb), half, :] = weights
            d_t[tile_of(qb, kb), half, :] = slope.astype(BF16)
            if diagonal:
                att[qb, half, :] = dot(weights, v_s[kb])
            else:
                att[qb, half, :] += dot(weights, v_s[kb])

    def finish(qb):
        for part in range(TOK // QT):
            half = slice(part * QT, (part + 1) * QT)
            total = att[qb, half, :]
            mean = jnp.mean(total, -1, keepdims=True)
            out_off[qb, half, :] = (total - mean).astype(BF16)
            out_m[qb, :, half] = to_line(mean)

        @pl.when(qb != block)
        def _():
            remote(out_off.at[qb], off_s.at[:, pl.ds(head, HD)], ex_s.at[3], ex_r.at[3], peer(qb)).start()
            remote(out_m.at[qb], m_s.at[block], ex_s.at[4], ex_r.at[4], peer(qb)).start()

    after, across, ahead = rem(block + 1, NC), rem(block + 2, NC), rem(block + 3, NC)
    tile(block, block, True)
    settle(q_s.at[pl.ds(0, 3)], ex_r.at[0])
    settle(q_s.at[pl.ds(0, 3)], ex_r.at[2])

    def diagonals(step, carry):
        b = rem(block + 1 + 2 * step, NC)
        tile(b, b, True)
        return carry

    def near_pairs(step, carry):
        one = jnp.where(step == 2, after, block)
        two = jnp.where(step == 0, after, ahead)
        tile(jnp.maximum(one, two), jnp.minimum(one, two), False)
        return carry

    lax.fori_loop(0, 2, diagonals, 0)
    lax.fori_loop(0, 3, near_pairs, 0)
    settle(q_s.at[pl.ds(0, 3)], ex_r.at[1])

    @pl.when(relay_away)
    def _():
        settle(og_mid, og_r.at[0])

    @pl.when(beyond_away)
    def _():
        remote(og_mid, og, og_s.at[1], og_r.at[1], device(held_x, y_at)).start()

    def near_rows(step, carry):
        qb = rem(block + 1 + 2 * step, NC)

        @pl.when(qb > across)
        def _():
            tile(qb, across, False)

        finish(qb)
        return carry

    lax.fori_loop(0, 2, near_rows, 0)
    tile(across, across, True)

    def far_row(kb, carry):
        tile(across, kb, False)
        return carry

    lax.fori_loop(0, across, far_row, 0)
    finish(across)

    @pl.when(block > across)
    def _():
        tile(block, across, False)

    finish(block)
    off_s[:, pl.ds(head, HD)] = out_off[block]
    m_s[block] = out_m[block]

    @pl.when(beyond_away)
    def _():
        settle(og, og_r.at[1])

    @pl.when(jnp.logical_not(beyond_away))
    def _():
        og[...] = og_mid[...]

    masked = jnp.where(slot_col >= 0.0, og[...], jnp.zeros((TOK, D), BF16))
    og[...] = masked
    gg[...] = dot(masked, ow[...], 1, 1)

    settle(off_s.at[:, pl.ds(0, 3 * HD)], ex_r.at[3])
    settle(m_s.at[pl.ds(0, 3)], ex_r.at[4])
    m_all = (m_s[0] + m_s[1] + m_s[2] + m_s[3]) * (1.0 / NC)
    for part in range(TOK // QT):
        half = slice(part * QT, (part + 1) * QT)
        off = off_s[half, :].astype(F32)
        gaps = [to_column((m_s[h] - m_all)[:, half]) for h in range(NC)]
        off = jnp.concatenate([off[:, h * HD:(h + 1) * HD] + gaps[h] for h in range(NC)], axis=1)
        deviation = off - jnp.mean(off, -1, keepdims=True)
        r_a = lax.rsqrt(jnp.mean(deviation * deviation, -1, keepdims=True) + EPSILON)
        a_norm = deviation * r_a
        an_s[half, :] = a_norm
        cot = gg[half, :] * gate_s[half, :].astype(F32)
        grad = r_a * (
            cot - jnp.mean(cot, -1, keepdims=True) - a_norm * jnp.mean(cot * a_norm, -1, keepdims=True)
        )
        grad = grad.astype(BF16)
        for j in range(NC):
            out_da[j, half, :] = grad[:, j * HD:(j + 1) * HD]
        for k in range(1, NC):
            j = each_peer(k)
            rows = pl.ds(part * QT, QT)
            remote(out_da.at[j, rows], da_s.at[block, rows], ex_s.at[5], ex_r.at[5], peer(j)).start()
    da_s[block] = out_da[block]

    a_norm = an_s[...]
    gated = (a_norm * gate_s[...].astype(F32)).astype(BF16)
    mix[...] = (emb[...].astype(F32) + dot(gated, ow[...])).astype(BF16)

    @pl.when(away)
    def _():
        remote(mix, mixed, mx_s, mx_r, device(held_x, held_y)).start()

    @pl.when(jnp.logical_not(away))
    def _():
        mixed[...] = mix[...]

    e_acc[...] = dot((gg[...] * a_norm * slopes[:, :D]).astype(BF16), pw[:, :D], 1, 1)
    for b in range(NC):
        q_t[b] = q_s[b].astype(F32).T.astype(BF16)

    def by_row(qb):
        grad = da_s[qb]
        dq_acc[...] = jnp.zeros((TOK, HD), F32)

        def tile(kb, carry):
            slope = dot(grad, v_s[kb], 1, 1)
            ds = (slope * d_t[tile_of(qb, kb)].astype(F32)).astype(BF16)
            d_t[tile_of(qb, kb)] = ds
            dq_acc[...] += dot(ds, k_s[kb])
            return carry

        lax.fori_loop(0, qb + 1, tile, 0)
        out_dq[qb] = dq_acc[...].astype(BF16)
        da_t[qb] = grad.astype(F32).T.astype(BF16)

    by_row(block)
    settle(da_s.at[pl.ds(0, 3)], ex_r.at[5])

    def other_row(k, carry):
        qb = each_peer(k)
        by_row(qb)
        remote(out_dq.at[qb], dqkv.at[:, pl.ds(head, HD)], ex_s.at[6], ex_r.at[6], peer(qb)).start()
        return carry

    lax.fori_loop(1, NC, other_row, 0)

    def by_column(step, carry):
        kb = rem(block + 1 + step, NC)
        d_kv[...] = jnp.zeros((2, HD, TOK), F32)

        def tile(qb, inner):
            d_kv[0] += dot(q_t[qb], d_t[tile_of(qb, kb)])
            d_kv[1] += dot(da_t[qb], w_t[tile_of(qb, kb)])
            return inner

        lax.fori_loop(kb, NC, tile, 0)
        out_dk[kb] = d_kv[0].T.astype(BF16)
        out_dv[kb] = d_kv[1].T.astype(BF16)

        @pl.when(kb != block)
        def _():
            remote(out_dk.at[kb], dqkv.at[:, pl.ds(D + head, HD)], ex_s.at[7], ex_r.at[7], peer(kb)).start()
            remote(out_dv.at[kb], dqkv.at[:, pl.ds(2 * D + head, HD)], ex_s.at[8], ex_r.at[8], peer(kb)).start()

        return carry

    lax.fori_loop(0, NC, by_column, 0)
    dqkv[:, pl.ds(head, HD)] = out_dq[block]
    dqkv[:, pl.ds(D + head, HD)] = out_dk[block]
    dqkv[:, pl.ds(2 * D + head, HD)] = out_dv[block]

    incoming = e_acc[...]
    for kind, part in ((6, 0), (7, 1), (8, 2)):
        settle(off_s.at[:, pl.ds(0, 3 * HD)], ex_r.at[kind])
        grad = dqkv[:, part * D:(part + 1) * D].astype(F32) * slopes[:, (part + 1) * D:(part + 2) * D]
        incoming = incoming + dot(grad.astype(BF16), pw[:, (part + 1) * D:(part + 2) * D], 1, 1)
    norm = normed[...]
    embed_grad = r_x[...] * (
        incoming
        - jnp.mean(incoming, -1, keepdims=True)
        - norm * jnp.mean(incoming * norm, -1, keepdims=True)
    ) + og[...].astype(F32)
    embed_grad = embed_grad.astype(BF16)

    for first in range(0, ND, GROUP):
        slots = iota((GROUP * CAP, TOK), 0) + first * CAP
        sorted_rows = dot(one_hot(slots == slot_line.astype(jnp.int32)), embed_grad)
        halves = [sorted_rows[:, :256].reshape(GROUP, CAP, 256), sorted_rows[:, 256:].reshape(GROUP, CAP, 256)]
        out2[first:first + GROUP] = jnp.concatenate(halves, axis=1).astype(BF16)
        for k in order_of(first):
            if k != HERE:
                remote(out2.at[k], recv2.at[opposite(k)], b_s, b_r, place(k)).start()
    recv2[HERE] = out2[HERE]

    @pl.when(relay_away)
    def _():
        settle(ask_mid, ids_s.at[0])

    @pl.when(jnp.logical_not(relay_away))
    def _():
        settle(ask_mid.at[pl.ds(0, 7)], ids_s.at[0])

    settle(ask_in.at[pl.ds(0, 120)], ids_s.at[1])
    settle(out1.at[pl.ds(0, ND - 1)], a_s)
    for kind in (0, 1, 2, 3, 5, 6, 7, 8):
        settle(out_q.at[pl.ds(0, 3)], ex_s.at[kind])
    settle(out_m.at[pl.ds(0, 3)], ex_s.at[4])

    @pl.when(relay_away)
    def _():
        settle(og_in, og_s.at[0])

    @pl.when(beyond_away)
    def _():
        settle(og_mid, og_s.at[1])

    @pl.when(away)
    def _():
        settle(v_out, ids_s.at[2])
        settle(mix, mx_s)
        settle(mixed, mx_r)

    settle(out2.at[pl.ds(0, ND - 1)], b_s)
    settle(recv2.at[pl.ds(0, ND - 1)], b_r)


def scatter_kernel(wrow, recv2, mix, out, mixed, rows):
    step = pl.program_id(0)

    @pl.when(step == 0)
    def _():
        for g in range(ND // GROUP):
            got = recv2[g * GROUP:(g + 1) * GROUP].astype(F32)
            rows[g * GROUP * CAP:(g + 1) * GROUP * CAP] = jnp.concatenate(
                [got[:, :CAP].reshape(GROUP * CAP, 256), got[:, CAP:].reshape(GROUP * CAP, 256)], axis=1
            ).astype(BF16)

    mixed[...] = mix[...]
    size = out.shape[0]
    wanted = wrow[...].astype(jnp.int32) - step * size
    for part in range(size // 256):
        at = slice(part * 256, (part + 1) * 256)
        out[at, :] = dot(one_hot(iota((256, SLOTS), 0) + part * 256 == wanted), rows[...])


def shards(owner, row, lengths, table, proj_weight, out_weight, out_grad):
    vmem = pl.BlockSpec(memory_space=pltpu.VMEM)
    hbm = pl.BlockSpec(memory_space=pltpu.HBM)
    V = pltpu.VMEM
    DMA = pltpu.SemaphoreType.DMA
    mixed, recv2, wrow = pl.pallas_call(
        layer,
        out_shape=(
            jax.ShapeDtypeStruct((TOK, D), BF16),
            jax.ShapeDtypeStruct((ND, 2 * CAP, 256), BF16),
            jax.ShapeDtypeStruct((1, SLOTS), F32),
        ),
        in_specs=[vmem, vmem, pl.BlockSpec(memory_space=pltpu.SMEM), hbm, hbm, hbm, hbm],
        out_specs=(vmem, vmem, vmem),
        scratch_shapes=[
            V((ROWS, D), BF16), V((D, 4 * D), BF16), V((D, D), BF16), V((TOK, D), BF16), V((TOK, D), BF16), V((TOK, D), BF16),
            V((1, 1, TOK), jnp.int32), V((1, 1, TOK), jnp.int32), V((8, 1, ND), F32), V((8, 1, ND), F32), V((ND, 1, ND), F32),
            V((ND, 2 * CAP, 256), BF16), V((ND, 2 * CAP, 256), BF16), V((TOK, D), BF16),
            V((TOK, D), F32), V((TOK, 1), F32), V((TOK, 4 * D), F32), V((TOK, D), BF16), V((TOK, D), F32),
        ] + [V((NC, TOK, HD), BF16)] * 12 + [
            V((TOK, D), BF16), V((TOK, 3 * D), BF16), V((NC, 1, TOK), F32), V((NC, 1, TOK), F32),
            V((TOK, D), F32), V((NC, TOK, HD), F32), V((10, TOK, TOK), BF16), V((10, TOK, TOK), BF16),
            V((NC, HD, TOK), BF16), V((NC, HD, TOK), BF16),
            V((TOK, HD), F32), V((2, HD, TOK), F32), V((TOK, D), F32), V((TOK, D), BF16),
            V((ND, 2 * CAP, 256), BF16),
            DMA((4,)), DMA((3,)), DMA((3,)), DMA((2,)), DMA((2,)), DMA, DMA, DMA((9,)), DMA((9,)), DMA, DMA, DMA, DMA,
        ],
        compiler_params=pltpu.CompilerParams(
            collective_id=0, has_side_effects=True, vmem_limit_bytes=52 * 1024 * 1024
        ),
    )(
        owner.reshape(1, TOK), row.reshape(1, TOK), lengths, table, proj_weight, out_weight,
        out_grad.reshape(TOK, D),
    )
    steps = 4
    table_grad, mixed = pl.pallas_call(
        scatter_kernel,
        grid=(steps,),
        out_shape=(jax.ShapeDtypeStruct((ROWS, D), F32), jax.ShapeDtypeStruct((TOK, D), BF16)),
        in_specs=[vmem, vmem, pl.BlockSpec((TOK // steps, D), lambda i: (i, 0))],
        out_specs=(
            pl.BlockSpec((ROWS // steps, D), lambda i: (i, 0)),
            pl.BlockSpec((TOK // steps, D), lambda i: (i, 0)),
        ),
        scratch_shapes=[V((SLOTS, D), BF16)],
        compiler_params=pltpu.CompilerParams(vmem_limit_bytes=32 * 1024 * 1024),
    )(wrow, recv2, mixed)
    return (mixed.reshape(1, TOK, D), table_grad)


def solution(mesh):
    placed = (
        P("user", "ctx", None),
        P("user", "ctx"),
        P("user"),
        P(("user", "ctx"), None),
        P(),
        P(),
        P("user", "ctx", None),
    )
    return jax.shard_map(
        shards,
        mesh=mesh,
        in_specs=placed,
        out_specs=(P("user", "ctx", None), P(("user", "ctx"), None)),
        check_vma=False,
    )
```

```python
import jax
import jax.numpy as jnp
from jax import lax
from jax.experimental import pallas as pl
from jax.experimental.pallas import tpu as pltpu
from jax.sharding import PartitionSpec as P

MESH = pl.DeviceIdType.MESH
F32 = jnp.float32
BF16 = jnp.bfloat16
NC = 4
ND = 128
TOK = 512
SEQ = 2048
D = 512
HD = 128
CAP = 8
ROWS = 2048
SLOTS = ND * CAP
GROUP = 32
EPSILON = 1e-05
SCALE = HD ** (-0.5)
QT = 256


def div(a, b):
    return lax.div(a, jnp.int32(b))


def rem(a, b):
    return lax.rem(a, jnp.int32(b))


SETS = sorted(((dy, dz) for dy in range(4) for dz in range(4)), key=lambda d: -((0, 1, 2, 1)[d[0]] + (0, 1, 2, 1)[d[1]]))
HERE = SETS.index((0, 0)) * 8


def opposite_set(k):
    return SETS.index(((4 - SETS[k][0]) % 4, (4 - SETS[k][1]) % 4))


def opposite_member(k):
    return k // 4 * 4 + (4 - k % 4) % 4


def opposite(k):
    return opposite_set(k // 8) * 8 + opposite_member(k % 8)


def order_of(first):
    far = (0, 1, 2, 1)
    return sorted(
        range(first, first + GROUP),
        key=lambda k: -(far[SETS[k // 8][0]] + far[SETS[k // 8][1]] + far[k % 4]),
    )


def iota(shape, axis):
    return lax.broadcasted_iota(jnp.int32, shape, axis)


def to_column(line):
    n = line.shape[1]
    eye = iota((n, n), 0) == iota((n, n), 1)
    return jnp.sum(jnp.where(eye, line, 0.0), axis=1, keepdims=True)


def to_line(column):
    n = column.shape[0]
    eye = iota((n, n), 0) == iota((n, n), 1)
    return jnp.sum(jnp.where(eye, column, 0.0), axis=0, keepdims=True)


def one_hot(match):
    return jnp.where(match, 1.0, 0.0).astype(BF16)


def dot(a, b, ca=1, cb=0):
    return lax.dot_general(a, b, (((ca,), (cb,)), ((), ())), preferred_element_type=F32)


def remote(src, dst, send, recv, target):
    return pltpu.make_async_remote_copy(
        src_ref=src, dst_ref=dst, send_sem=send, recv_sem=recv, device_id=target, device_id_type=MESH
    )


def tile_of(q, k):
    return div(q * (q + 1), 2) + k


def settle(view, sem):
    pltpu.make_async_copy(view, view, sem).wait()


def silu_parts(values):
    half = values * 0.5
    t = jnp.tanh(half)
    turned = half * t
    return half + turned, (0.5 + 0.5 * t) * (1.0 + (half - turned))


def layer(
    owner_h, row_h, length, table_h, pw_h, ow_h, og_h,
    mixed, recv2, wrow,
    owner, row, table, pw, ow, og, og_in, og_mid, v_out, v_held, ask_out, ask_mid, ask_in, out1, recv1, emb, normed, r_x, slopes, gate_s, gg,
    out_q, out_k, out_v, out_off, out_da, out_dk, out_dv, out_dq, q_s, k_s, v_s, da_s, off_s, dqkv, out_m, m_s,
    an_s, att, w_t, d_t, da_t, q_t, dq_acc, d_kv, e_acc, mix, out2,
    load, ids_s, ids_r, og_s, og_r, a_s, a_r, ex_s, ex_r, mx_s, mx_r, b_s, b_r,
):
    user, ctx = lax.axis_index("user"), lax.axis_index("ctx")
    core, z_at, y_at = rem(user, 2), rem(div(user, 2), 4), div(user, 8)

    def device(x, y, z=z_at, c=core):
        return ((y * 4 + z) * 2 + c, x)

    xs = [rem(ctx + d, 4) for d in range(4)]
    ys = [rem(y_at + d, 4) for d in range(4)]
    zs = [rem(z_at + d, 4) for d in range(4)]
    cores = [core, 1 - core]

    def place(k):
        dy, dz = SETS[k // 8]
        return device(xs[k % 4], ys[dy], zs[dz], cores[k % 8 // 4])

    work_x, work_y = ctx + core * (y_at - ctx), y_at + core * (rem(ctx + y_at, 4) - y_at)
    back = rem(y_at + 4 - ctx, 4)
    held_x, held_y = ctx + core * (back - ctx), y_at + core * (ctx - y_at)
    block = held_x
    away = jnp.logical_or(work_x != ctx, work_y != y_at)
    relay_away, beyond_away = work_y != y_at, held_x != ctx

    def peer(j):
        other = (rem(j + ctx, 4) * 4 + z_at) * 2 + 1
        return (user + core * (other - user), j + core * (ctx - j))

    def each_peer(k):
        return rem(block + k, NC)

    barrier = pltpu.get_barrier_semaphore()

    head = pl.multiple_of(block * HD, HD)
    loads = [
        pltpu.make_async_copy(og_h, og_in, load.at[0]),
        pltpu.make_async_copy(table_h, table, load.at[1]),
        pltpu.make_async_copy(ow_h, ow, load.at[2]),
        pltpu.make_async_copy(pw_h, pw, load.at[3]),
        pltpu.make_async_copy(owner_h, owner, load.at[4]),
        pltpu.make_async_copy(row_h, row, load.at[5]),
    ]
    for copy in reversed(loads):
        copy.start()

    for k in range(ND):
        if k != HERE:
            pl.semaphore_signal(barrier, inc=1, device_id=place(k), device_id_type=MESH)

    loads[4].wait()
    loads[5].wait()

    places = ctx * TOK + iota((1, TOK), 1)
    valid = places < length[0]
    who = owner[...]
    far_x = jnp.bitwise_and(who + (4 - work_x), 3)
    far_core = jnp.bitwise_and(lax.shift_right_logical(who, 2) + core, 1)
    far_z = jnp.bitwise_and(lax.shift_right_logical(who, 3) + (4 - z_at), 3)
    far_y = jnp.bitwise_and(lax.shift_right_logical(who, 5) + (4 - work_y), 3)
    far_set = jnp.zeros((1, TOK), jnp.int32)
    for number, (dy, dz) in enumerate(SETS):
        far_set = jnp.where(far_y * 4 + far_z == dy * 4 + dz, number, far_set)
    own = jnp.where(valid, far_set * 8 + far_core * 4 + far_x, -1)
    match = iota((ND, TOK), 0) == own
    before = one_hot(iota((TOK, TOK), 0) < iota((TOK, TOK), 1))
    rank = dot(one_hot(match), before)
    slot = jnp.sum(jnp.where(match, rank, 0.0), axis=0, keepdims=True).astype(jnp.int32)
    slot_own = jnp.where(valid, own * CAP + slot, -1)
    v_out[0] = slot_own

    lane_own = jnp.where(valid, lax.shift_right_arithmetic(own, 3) * CAP + slot, -1)
    lanes_hot = one_hot(iota((TOK, ND), 1) == to_column(lane_own.astype(F32)).astype(jnp.int32))
    sub16 = iota((16, TOK), 0)
    digits = jnp.where(sub16 < 8, lax.shift_right_arithmetic(row[...] + 1, 6), jnp.bitwise_and(row[...] + 1, 63))
    digits = jnp.where(jnp.bitwise_and(sub16, 7) == far_core * 4 + far_x, digits, 0).astype(F32).astype(BF16)
    lines = dot(digits, lanes_hot)
    lines = lines[:8] * 64.0 + lines[8:]
    for member in range(8):
        ask_out[member] = lines[member:member + 1]

    pl.semaphore_wait(barrier, ND - 1)

    for member in range(8):
        line_x, line_core = rem(work_x + member % 4, 4), rem(core + member // 4, 2)
        here = jnp.logical_and(jnp.logical_and(line_x == ctx, line_core == core), work_y == y_at)

        @pl.when(jnp.logical_not(here))
        def _():
            target = device(line_x, work_y, z_at, line_core)
            line = ask_mid.at[opposite_member(member)]
            remote(ask_out.at[member], line, ids_s.at[0], ids_r.at[0], target).start()

        @pl.when(here)
        def _():
            ask_mid[opposite_member(member)] = ask_out[member]

    @pl.when(away)
    def _():
        remote(v_out, v_held, ids_s.at[2], ids_r.at[2], device(work_x, work_y)).start()

    @pl.when(jnp.logical_not(away))
    def _():
        v_held[0] = slot_own

    loads[0].wait()

    @pl.when(relay_away)
    def _():
        remote(og_in, og_mid, og_s.at[0], og_r.at[0], device(ctx, work_y)).start()

    @pl.when(jnp.logical_not(relay_away))
    def _():
        og_mid[...] = og_in[...]

    @pl.when(relay_away)
    def _():
        settle(ask_mid, ids_r.at[0])

    @pl.when(jnp.logical_not(relay_away))
    def _():
        settle(ask_mid.at[pl.ds(0, 7)], ids_r.at[0])

    for number in range(16):
        if number * 8 != HERE:
            lines = ask_in.at[pl.ds(opposite_set(number) * 8, 8)]
            remote(ask_mid, lines, ids_s.at[1], ids_r.at[1], place(number * 8)).start()
    ask_in[HERE:HERE + 8] = ask_mid[...]
    settle(ask_in.at[pl.ds(0, 120)], ids_r.at[1])
    loads[1].wait()

    for first in range(0, ND, GROUP):
        wanted = []
        for number in range(first // 8, (first + GROUP) // 8):
            mine = iota((1, CAP, ND), 2) == iota((1, CAP, ND), 1) + opposite_set(number) * CAP
            lines = jnp.where(mine, ask_in[number * 8:number * 8 + 8], 0.0)
            wanted.append(jnp.sum(lines, axis=2, keepdims=True).reshape(8 * CAP, 1))
        wanted = jnp.concatenate(wanted, axis=0) - 1.0
        wrow[:, first * CAP:(first + GROUP) * CAP] = to_line(wanted)
        found = dot(one_hot(iota((GROUP * CAP, ROWS), 1) == wanted.astype(jnp.int32)), table[...])
        halves = [found[:, :256].reshape(GROUP, CAP, 256), found[:, 256:].reshape(GROUP, CAP, 256)]
        out1[first:first + GROUP] = jnp.concatenate(halves, axis=1).astype(BF16)
        for k in order_of(first):
            if k != HERE:
                remote(out1.at[k], recv1.at[opposite(k)], a_s, a_r, place(k)).start()
    recv1[HERE] = out1[HERE]

    @pl.when(away)
    def _():
        settle(v_held, ids_r.at[2])

    slot_line = v_held[0].astype(F32)
    slot_col = to_column(slot_line)
    loads[2].wait()
    loads[3].wait()

    settle(recv1.at[pl.ds(0, ND - 1)], a_r)
    embed = jnp.zeros((TOK, D), F32)
    for g in range(ND // GROUP):
        got = recv1[g * GROUP:(g + 1) * GROUP].astype(F32)
        rows = jnp.concatenate(
            [got[:, :CAP].reshape(GROUP * CAP, 256), got[:, CAP:].reshape(GROUP * CAP, 256)], axis=1
        ).astype(BF16)
        lanes = iota((TOK, GROUP * CAP), 1) + g * GROUP * CAP
        embed = embed + dot(one_hot(lanes == slot_col.astype(jnp.int32)), rows)
    emb[...] = embed.astype(BF16)
    center = jnp.mean(embed, -1, keepdims=True)
    deviation = embed - center
    inverse = lax.rsqrt(jnp.mean(deviation * deviation, -1, keepdims=True) + EPSILON)
    norm = deviation * inverse
    normed[...] = norm
    r_x[...] = inverse
    norm_low = norm.astype(BF16)

    for kind, (outbox, inbox) in enumerate(((out_q, q_s), (out_k, k_s), (out_v, v_s))):
        part = slice((kind + 1) * D, (kind + 2) * D)
        silu, slope = silu_parts(dot(norm_low, pw[:, part]))
        slopes[:, part] = slope
        low = silu.astype(BF16)
        for j in range(NC):
            outbox[j] = low[:, j * HD:(j + 1) * HD]
        inbox[block] = outbox[block]
    def hand_on(k):
        j = each_peer(k)
        for outbox, inbox in ((out_q, q_s), (out_k, k_s), (out_v, v_s)):
            remote(outbox.at[j], inbox.at[block], ex_s.at[k - 1], ex_r.at[k - 1], peer(j)).start()

    hand_on(1)
    hand_on(3)

    silu, slope = silu_parts(dot(norm_low, pw[:, :D]))
    slopes[:, :D] = slope
    gate_s[...] = silu.astype(BF16)

    def tile(qb, kb, diagonal):
        for part in range(TOK // QT):
            half = slice(part * QT, (part + 1) * QT)
            half_score = dot(q_s[qb, half, :], k_s[kb], 1, 1) * (0.5 * SCALE)
            t = jnp.tanh(half_score)
            turned = half_score * t
            weights = half_score + turned
            slope = (1.0 + t) * ((1.0 + half_score) - turned) * (0.5 * SCALE)
            if diagonal:
                allowed = (iota((QT, TOK), 1) - iota((QT, TOK), 0)) <= part * QT
                weights = jnp.where(allowed, weights, 0.0)
                slope = jnp.where(allowed, slope, 0.0)
            weights = weights.astype(BF16)
            w_t[tile_of(qb, kb), half, :] = weights
            d_t[tile_of(qb, kb), half, :] = slope.astype(BF16)
            if diagonal:
                att[qb, half, :] = dot(weights, v_s[kb])
            else:
                att[qb, half, :] += dot(weights, v_s[kb])

    def finish(qb):
        for part in range(TOK // QT):
            half = slice(part * QT, (part + 1) * QT)
            total = att[qb, half, :]
            mean = jnp.mean(total, -1, keepdims=True)
            out_off[qb, half, :] = (total - mean).astype(BF16)
            out_m[qb, :, half] = to_line(mean)

        @pl.when(qb != block)
        def _():
            remote(out_off.at[qb], off_s.at[:, pl.ds(head, HD)], ex_s.at[3], ex_r.at[3], peer(qb)).start()
            remote(out_m.at[qb], m_s.at[block], ex_s.at[4], ex_r.at[4], peer(qb)).start()

    after, across, ahead = rem(block + 1, NC), rem(block + 2, NC), rem(block + 3, NC)
    tile(block, block, True)
    settle(out_q.at[pl.ds(0, 3)], ex_s.at[0])
    settle(out_q.at[pl.ds(0, 3)], ex_s.at[2])
    hand_on(2)
    settle(q_s.at[pl.ds(0, 3)], ex_r.at[0])
    settle(q_s.at[pl.ds(0, 3)], ex_r.at[2])

    def diagonals(step, carry):
        b = rem(block + 1 + 2 * step, NC)
        tile(b, b, True)
        return carry

    def near_pairs(step, carry):
        one = jnp.where(step == 2, after, block)
        two = jnp.where(step == 0, after, ahead)
        tile(jnp.maximum(one, two), jnp.minimum(one, two), False)
        return carry

    lax.fori_loop(0, 2, diagonals, 0)
    lax.fori_loop(0, 3, near_pairs, 0)
    settle(q_s.at[pl.ds(0, 3)], ex_r.at[1])

    @pl.when(relay_away)
    def _():
        settle(og_mid, og_r.at[0])

    @pl.when(beyond_away)
    def _():
        remote(og_mid, og, og_s.at[1], og_r.at[1], device(held_x, y_at)).start()

    def near_rows(step, carry):
        qb = rem(block + 1 + 2 * step, NC)

        @pl.when(qb > across)
        def _():
            tile(qb, across, False)

        finish(qb)
        return carry

    lax.fori_loop(0, 2, near_rows, 0)
    tile(across, across, True)

    def far_row(kb, carry):
        tile(across, kb, False)
        return carry

    lax.fori_loop(0, across, far_row, 0)
    finish(across)

    @pl.when(block > across)
    def _():
        tile(block, across, False)

    finish(block)
    off_s[:, pl.ds(head, HD)] = out_off[block]
    m_s[block] = out_m[block]

    @pl.when(beyond_away)
    def _():
        settle(og, og_r.at[1])

    @pl.when(jnp.logical_not(beyond_away))
    def _():
        og[...] = og_mid[...]

    masked = jnp.where(slot_col >= 0.0, og[...], jnp.zeros((TOK, D), BF16))
    og[...] = masked
    gg[...] = dot(masked, ow[...], 1, 1)

    settle(off_s.at[:, pl.ds(0, 3 * HD)], ex_r.at[3])
    settle(m_s.at[pl.ds(0, 3)], ex_r.at[4])
    m_all = (m_s[0] + m_s[1] + m_s[2] + m_s[3]) * (1.0 / NC)
    for part in range(TOK // QT):
        half = slice(part * QT, (part + 1) * QT)
        off = off_s[half, :].astype(F32)
        gaps = [to_column((m_s[h] - m_all)[:, half]) for h in range(NC)]
        off = jnp.concatenate([off[:, h * HD:(h + 1) * HD] + gaps[h] for h in range(NC)], axis=1)
        deviation = off - jnp.mean(off, -1, keepdims=True)
        r_a = lax.rsqrt(jnp.mean(deviation * deviation, -1, keepdims=True) + EPSILON)
        a_norm = deviation * r_a
        an_s[half, :] = a_norm
        cot = gg[half, :] * gate_s[half, :].astype(F32)
        grad = r_a * (
            cot - jnp.mean(cot, -1, keepdims=True) - a_norm * jnp.mean(cot * a_norm, -1, keepdims=True)
        )
        grad = grad.astype(BF16)
        for j in range(NC):
            out_da[j, half, :] = grad[:, j * HD:(j + 1) * HD]
        for k in range(1, NC):
            j = each_peer(k)
            rows = pl.ds(part * QT, QT)
            remote(out_da.at[j, rows], da_s.at[block, rows], ex_s.at[5], ex_r.at[5], peer(j)).start()
    da_s[block] = out_da[block]

    a_norm = an_s[...]
    gated = (a_norm * gate_s[...].astype(F32)).astype(BF16)
    mix[...] = (emb[...].astype(F32) + dot(gated, ow[...])).astype(BF16)

    @pl.when(away)
    def _():
        remote(mix, mixed, mx_s, mx_r, device(held_x, held_y)).start()

    @pl.when(jnp.logical_not(away))
    def _():
        mixed[...] = mix[...]

    e_acc[...] = dot((gg[...] * a_norm * slopes[:, :D]).astype(BF16), pw[:, :D], 1, 1)
    for b in range(NC):
        q_t[b] = q_s[b].astype(F32).T.astype(BF16)

    def by_row(qb):
        grad = da_s[qb]
        dq_acc[...] = jnp.zeros((TOK, HD), F32)

        def tile(kb, carry):
            slope = dot(grad, v_s[kb], 1, 1)
            ds = (slope * d_t[tile_of(qb, kb)].astype(F32)).astype(BF16)
            d_t[tile_of(qb, kb)] = ds
            dq_acc[...] += dot(ds, k_s[kb])
            return carry

        lax.fori_loop(0, qb + 1, tile, 0)
        out_dq[qb] = dq_acc[...].astype(BF16)
        da_t[qb] = grad.astype(F32).T.astype(BF16)

    by_row(block)
    settle(da_s.at[pl.ds(0, 3)], ex_r.at[5])

    def other_row(k, carry):
        qb = each_peer(k)
        by_row(qb)
        remote(out_dq.at[qb], dqkv.at[:, pl.ds(head, HD)], ex_s.at[6], ex_r.at[6], peer(qb)).start()
        return carry

    lax.fori_loop(1, NC, other_row, 0)

    def by_column(step, carry):
        kb = rem(block + 1 + step, NC)
        d_kv[...] = jnp.zeros((2, HD, TOK), F32)

        def tile(qb, inner):
            d_kv[0] += dot(q_t[qb], d_t[tile_of(qb, kb)])
            d_kv[1] += dot(da_t[qb], w_t[tile_of(qb, kb)])
            return inner

        lax.fori_loop(kb, NC, tile, 0)
        out_dk[kb] = d_kv[0].T.astype(BF16)
        out_dv[kb] = d_kv[1].T.astype(BF16)

        @pl.when(kb != block)
        def _():
            remote(out_dk.at[kb], dqkv.at[:, pl.ds(D + head, HD)], ex_s.at[7], ex_r.at[7], peer(kb)).start()
            remote(out_dv.at[kb], dqkv.at[:, pl.ds(2 * D + head, HD)], ex_s.at[8], ex_r.at[8], peer(kb)).start()

        return carry

    lax.fori_loop(0, NC, by_column, 0)
    dqkv[:, pl.ds(head, HD)] = out_dq[block]
    dqkv[:, pl.ds(D + head, HD)] = out_dk[block]
    dqkv[:, pl.ds(2 * D + head, HD)] = out_dv[block]

    incoming = e_acc[...]
    for kind, part in ((6, 0), (7, 1), (8, 2)):
        settle(off_s.at[:, pl.ds(0, 3 * HD)], ex_r.at[kind])
        grad = dqkv[:, part * D:(part + 1) * D].astype(F32) * slopes[:, (part + 1) * D:(part + 2) * D]
        incoming = incoming + dot(grad.astype(BF16), pw[:, (part + 1) * D:(part + 2) * D], 1, 1)
    norm = normed[...]
    embed_grad = r_x[...] * (
        incoming
        - jnp.mean(incoming, -1, keepdims=True)
        - norm * jnp.mean(incoming * norm, -1, keepdims=True)
    ) + og[...].astype(F32)
    embed_grad = embed_grad.astype(BF16)

    for first in range(0, ND, GROUP):
        slots = iota((GROUP * CAP, TOK), 0) + first * CAP
        sorted_rows = dot(one_hot(slots == slot_line.astype(jnp.int32)), embed_grad)
        halves = [sorted_rows[:, :256].reshape(GROUP, CAP, 256), sorted_rows[:, 256:].reshape(GROUP, CAP, 256)]
        out2[first:first + GROUP] = jnp.concatenate(halves, axis=1).astype(BF16)
        for k in order_of(first):
            if k != HERE:
                remote(out2.at[k], recv2.at[opposite(k)], b_s, b_r, place(k)).start()
    recv2[HERE] = out2[HERE]

    @pl.when(relay_away)
    def _():
        settle(ask_mid, ids_s.at[0])

    @pl.when(jnp.logical_not(relay_away))
    def _():
        settle(ask_mid.at[pl.ds(0, 7)], ids_s.at[0])

    settle(ask_in.at[pl.ds(0, 120)], ids_s.at[1])
    settle(out1.at[pl.ds(0, ND - 1)], a_s)
    for kind in (1, 3, 5, 6, 7, 8):
        settle(out_q.at[pl.ds(0, 3)], ex_s.at[kind])
    settle(out_m.at[pl.ds(0, 3)], ex_s.at[4])

    @pl.when(relay_away)
    def _():
        settle(og_in, og_s.at[0])

    @pl.when(beyond_away)
    def _():
        settle(og_mid, og_s.at[1])

    @pl.when(away)
    def _():
        settle(v_out, ids_s.at[2])
        settle(mix, mx_s)
        settle(mixed, mx_r)

    settle(out2.at[pl.ds(0, ND - 1)], b_s)
    settle(recv2.at[pl.ds(0, ND - 1)], b_r)


def scatter_kernel(wrow, recv2_h, mix, out, mixed, rows, recv2, load):
    step = pl.program_id(0)

    @pl.when(step == 0)
    def _():
        copies = []
        for g in range(ND // GROUP):
            part = pl.ds(g * GROUP, GROUP)
            copies.append(pltpu.make_async_copy(recv2_h.at[part], recv2.at[part], load.at[g]))
            copies[g].start()
        for g in range(ND // GROUP):
            copies[g].wait()
            got = recv2[g * GROUP:(g + 1) * GROUP].astype(F32)
            rows[g * GROUP * CAP:(g + 1) * GROUP * CAP] = jnp.concatenate(
                [got[:, :CAP].reshape(GROUP * CAP, 256), got[:, CAP:].reshape(GROUP * CAP, 256)], axis=1
            ).astype(BF16)

    mixed[...] = mix[...]
    size = out.shape[0]
    wanted = wrow[...].astype(jnp.int32) - step * size
    for part in range(size // 256):
        at = slice(part * 256, (part + 1) * 256)
        out[at, :] = dot(one_hot(iota((256, SLOTS), 0) + part * 256 == wanted), rows[...])


def shards(owner, row, lengths, table, proj_weight, out_weight, out_grad):
    vmem = pl.BlockSpec(memory_space=pltpu.VMEM)
    hbm = pl.BlockSpec(memory_space=pltpu.HBM)
    V = pltpu.VMEM
    DMA = pltpu.SemaphoreType.DMA
    mixed, recv2, wrow = pl.pallas_call(
        layer,
        out_shape=(
            jax.ShapeDtypeStruct((TOK, D), BF16),
            jax.ShapeDtypeStruct((ND, 2 * CAP, 256), BF16),
            jax.ShapeDtypeStruct((1, SLOTS), F32),
        ),
        in_specs=[hbm, hbm, pl.BlockSpec(memory_space=pltpu.SMEM), hbm, hbm, hbm, hbm],
        out_specs=(vmem, vmem, vmem),
        scratch_shapes=[
            V((1, TOK), jnp.int32), V((1, TOK), jnp.int32), V((ROWS, D), BF16), V((D, 4 * D), BF16), V((D, D), BF16), V((TOK, D), BF16), V((TOK, D), BF16), V((TOK, D), BF16),
            V((1, 1, TOK), jnp.int32), V((1, 1, TOK), jnp.int32), V((8, 1, ND), F32), V((8, 1, ND), F32), V((ND, 1, ND), F32),
            V((ND, 2 * CAP, 256), BF16), V((ND, 2 * CAP, 256), BF16), V((TOK, D), BF16),
            V((TOK, D), F32), V((TOK, 1), F32), V((TOK, 4 * D), F32), V((TOK, D), BF16), V((TOK, D), F32),
        ] + [V((NC, TOK, HD), BF16)] * 12 + [
            V((TOK, D), BF16), V((TOK, 3 * D), BF16), V((NC, 1, TOK), F32), V((NC, 1, TOK), F32),
            V((TOK, D), F32), V((NC, TOK, HD), F32), V((10, TOK, TOK), BF16), V((10, TOK, TOK), BF16),
            V((NC, HD, TOK), BF16), V((NC, HD, TOK), BF16),
            V((TOK, HD), F32), V((2, HD, TOK), F32), V((TOK, D), F32), V((TOK, D), BF16),
            V((ND, 2 * CAP, 256), BF16),
            DMA((6,)), DMA((3,)), DMA((3,)), DMA((2,)), DMA((2,)), DMA, DMA, DMA((9,)), DMA((9,)), DMA, DMA, DMA, DMA,
        ],
        compiler_params=pltpu.CompilerParams(
            collective_id=0, has_side_effects=True, vmem_limit_bytes=63 * 1024 * 1024
        ),
    )(
        owner.reshape(1, TOK), row.reshape(1, TOK), lengths, table, proj_weight, out_weight,
        out_grad.reshape(TOK, D),
    )
    steps = 4
    table_grad, mixed = pl.pallas_call(
        scatter_kernel,
        grid=(steps,),
        out_shape=(jax.ShapeDtypeStruct((ROWS, D), F32), jax.ShapeDtypeStruct((TOK, D), BF16)),
        in_specs=[vmem, hbm, pl.BlockSpec((TOK // steps, D), lambda i: (i, 0))],
        out_specs=(
            pl.BlockSpec((ROWS // steps, D), lambda i: (i, 0)),
            pl.BlockSpec((TOK // steps, D), lambda i: (i, 0)),
        ),
        scratch_shapes=[V((SLOTS, D), BF16), V((ND, 2 * CAP, 256), BF16), DMA((ND // GROUP,))],
        compiler_params=pltpu.CompilerParams(vmem_limit_bytes=63 * 1024 * 1024),
    )(wrow, recv2, mixed)
    return (mixed.reshape(1, TOK, D), table_grad)


def solution(mesh):
    placed = (
        P("user", "ctx", None),
        P("user", "ctx"),
        P("user"),
        P(("user", "ctx"), None),
        P(),
        P(),
        P("user", "ctx", None),
    )
    return jax.shard_map(
        shards,
        mesh=mesh,
        in_specs=placed,
        out_specs=(P("user", "ctx", None), P(("user", "ctx"), None)),
        check_vma=False,
    )
```

```python
import jax
import jax.numpy as jnp
from jax import lax
from jax.experimental import pallas as pl
from jax.experimental.pallas import tpu as pltpu
from jax.sharding import PartitionSpec as P

MESH = pl.DeviceIdType.MESH
F32 = jnp.float32
BF16 = jnp.bfloat16
NC = 4
ND = 128
TOK = 512
SEQ = 2048
D = 512
HD = 128
CAP = 8
ROWS = 2048
SLOTS = ND * CAP
GROUP = 32
EPSILON = 1e-05
SCALE = HD ** (-0.5)
QT = 256


def div(a, b):
    return lax.div(a, jnp.int32(b))


def rem(a, b):
    return lax.rem(a, jnp.int32(b))


SETS = sorted(((dy, dz) for dy in range(4) for dz in range(4)), key=lambda d: -((0, 1, 2, 1)[d[0]] + (0, 1, 2, 1)[d[1]]))
HERE = SETS.index((0, 0)) * 8


def opposite_set(k):
    return SETS.index(((4 - SETS[k][0]) % 4, (4 - SETS[k][1]) % 4))


def opposite_member(k):
    return k // 4 * 4 + (4 - k % 4) % 4


def opposite(k):
    return opposite_set(k // 8) * 8 + opposite_member(k % 8)


def order_of(first):
    far = (0, 1, 2, 1)
    return sorted(
        range(first, first + GROUP),
        key=lambda k: -(far[SETS[k // 8][0]] + far[SETS[k // 8][1]] + far[k % 4]),
    )


def iota(shape, axis):
    return lax.broadcasted_iota(jnp.int32, shape, axis)


def to_column(line):
    n = line.shape[1]
    eye = iota((n, n), 0) == iota((n, n), 1)
    return jnp.sum(jnp.where(eye, line, 0.0), axis=1, keepdims=True)


def to_line(column):
    n = column.shape[0]
    eye = iota((n, n), 0) == iota((n, n), 1)
    return jnp.sum(jnp.where(eye, column, 0.0), axis=0, keepdims=True)


def one_hot(match):
    return jnp.where(match, 1.0, 0.0).astype(BF16)


def dot(a, b, ca=1, cb=0):
    return lax.dot_general(a, b, (((ca,), (cb,)), ((), ())), preferred_element_type=F32)


def remote(src, dst, send, recv, target):
    return pltpu.make_async_remote_copy(
        src_ref=src, dst_ref=dst, send_sem=send, recv_sem=recv, device_id=target, device_id_type=MESH
    )


def tile_of(q, k):
    return div(q * (q + 1), 2) + k


def settle(view, sem):
    pltpu.make_async_copy(view, view, sem).wait()


def silu_parts(values):
    half = values * 0.5
    t = jnp.tanh(half)
    turned = half * t
    return half + turned, (0.5 + 0.5 * t) * (1.0 + (half - turned))


def layer(
    owner_h, row_h, length, table_h, pw_h, ow_h, og_h,
    mixed, recv2, wrow,
    owner, row, table, pw, ow, og, og_in, og_mid, v_out, v_held, ask_out, ask_mid, ask_in, out1, recv1, emb, normed, r_x, slopes, gate_s, gg,
    out_q, out_k, out_v, out_off, out_da, out_dk, out_dv, out_dq, q_s, k_s, v_s, da_s, off_s, dqkv, out_m, m_s,
    an_s, att, w_t, d_t, da_t, q_t, dq_acc, d_kv, e_acc, mix, out2,
    load, ids_s, ids_r, og_s, og_r, a_s, a_r, ex_s, ex_r, mx_s, mx_r, b_s, b_r,
):
    user, ctx = lax.axis_index("user"), lax.axis_index("ctx")
    core, z_at, y_at = rem(user, 2), rem(div(user, 2), 4), div(user, 8)

    def device(x, y, z=z_at, c=core):
        return ((y * 4 + z) * 2 + c, x)

    xs = [rem(ctx + d, 4) for d in range(4)]
    ys = [rem(y_at + d, 4) for d in range(4)]
    zs = [rem(z_at + d, 4) for d in range(4)]
    cores = [core, 1 - core]

    def place(k):
        dy, dz = SETS[k // 8]
        return device(xs[k % 4], ys[dy], zs[dz], cores[k % 8 // 4])

    work_x, work_y = ctx + core * (y_at - ctx), y_at + core * (rem(ctx + y_at, 4) - y_at)
    back = rem(y_at + 4 - ctx, 4)
    held_x, held_y = ctx + core * (back - ctx), y_at + core * (ctx - y_at)
    block = held_x
    away = jnp.logical_or(work_x != ctx, work_y != y_at)
    relay_away, beyond_away = work_y != y_at, held_x != ctx

    def peer(j):
        other = (rem(j + ctx, 4) * 4 + z_at) * 2 + 1
        return (user + core * (other - user), j + core * (ctx - j))

    def each_peer(k):
        return rem(block + k, NC)

    barrier = pltpu.get_barrier_semaphore()

    head = pl.multiple_of(block * HD, HD)
    loads = [
        pltpu.make_async_copy(og_h, og_in, load.at[0]),
        pltpu.make_async_copy(table_h, table, load.at[1]),
        pltpu.make_async_copy(ow_h, ow, load.at[2]),
        pltpu.make_async_copy(pw_h, pw, load.at[3]),
        pltpu.make_async_copy(owner_h, owner, load.at[4]),
        pltpu.make_async_copy(row_h, row, load.at[5]),
    ]
    for copy in reversed(loads):
        copy.start()

    for k in range(ND):
        if k != HERE:
            pl.semaphore_signal(barrier, inc=1, device_id=place(k), device_id_type=MESH)

    loads[4].wait()
    loads[5].wait()

    places = ctx * TOK + iota((1, TOK), 1)
    valid = places < length[0]
    who = owner[...]
    far_x = jnp.bitwise_and(who + (4 - work_x), 3)
    far_core = jnp.bitwise_and(lax.shift_right_logical(who, 2) + core, 1)
    far_z = jnp.bitwise_and(lax.shift_right_logical(who, 3) + (4 - z_at), 3)
    far_y = jnp.bitwise_and(lax.shift_right_logical(who, 5) + (4 - work_y), 3)
    far_set = jnp.zeros((1, TOK), jnp.int32)
    for number, (dy, dz) in enumerate(SETS):
        far_set = jnp.where(far_y * 4 + far_z == dy * 4 + dz, number, far_set)
    own = jnp.where(valid, far_set * 8 + far_core * 4 + far_x, -1)
    match = iota((ND, TOK), 0) == own
    before = one_hot(iota((TOK, TOK), 0) < iota((TOK, TOK), 1))
    rank = dot(one_hot(match), before)
    slot = jnp.sum(jnp.where(match, rank, 0.0), axis=0, keepdims=True).astype(jnp.int32)
    slot_own = jnp.where(valid, own * CAP + slot, -1)
    v_out[0] = slot_own

    lane_own = jnp.where(valid, lax.shift_right_arithmetic(own, 3) * CAP + slot, -1)
    lanes_hot = one_hot(iota((TOK, ND), 1) == to_column(lane_own.astype(F32)).astype(jnp.int32))
    sub16 = iota((16, TOK), 0)
    digits = jnp.where(sub16 < 8, lax.shift_right_arithmetic(row[...] + 1, 6), jnp.bitwise_and(row[...] + 1, 63))
    digits = jnp.where(jnp.bitwise_and(sub16, 7) == far_core * 4 + far_x, digits, 0).astype(F32).astype(BF16)
    lines = dot(digits, lanes_hot)
    lines = lines[:8] * 64.0 + lines[8:]
    for member in range(8):
        ask_out[member] = lines[member:member + 1]

    pl.semaphore_wait(barrier, ND - 1)

    for member in range(8):
        line_x, line_core = rem(work_x + member % 4, 4), rem(core + member // 4, 2)
        here = jnp.logical_and(jnp.logical_and(line_x == ctx, line_core == core), work_y == y_at)

        @pl.when(jnp.logical_not(here))
        def _():
            target = device(line_x, work_y, z_at, line_core)
            line = ask_mid.at[opposite_member(member)]
            remote(ask_out.at[member], line, ids_s.at[0], ids_r.at[0], target).start()

        @pl.when(here)
        def _():
            ask_mid[opposite_member(member)] = ask_out[member]

    @pl.when(away)
    def _():
        remote(v_out, v_held, ids_s.at[2], ids_r.at[2], device(work_x, work_y)).start()

    @pl.when(jnp.logical_not(away))
    def _():
        v_held[0] = slot_own

    loads[0].wait()

    @pl.when(relay_away)
    def _():
        remote(og_in, og_mid, og_s.at[0], og_r.at[0], device(ctx, work_y)).start()

    @pl.when(jnp.logical_not(relay_away))
    def _():
        og_mid[...] = og_in[...]

    @pl.when(relay_away)
    def _():
        settle(ask_mid, ids_r.at[0])

    @pl.when(jnp.logical_not(relay_away))
    def _():
        settle(ask_mid.at[pl.ds(0, 7)], ids_r.at[0])

    for number in range(16):
        if number * 8 != HERE:
            lines = ask_in.at[pl.ds(opposite_set(number) * 8, 8)]
            remote(ask_mid, lines, ids_s.at[1], ids_r.at[1], place(number * 8)).start()
    ask_in[HERE:HERE + 8] = ask_mid[...]
    settle(ask_in.at[pl.ds(0, 120)], ids_r.at[1])
    loads[1].wait()

    for first in range(0, ND, GROUP):
        wanted = []
        for number in range(first // 8, (first + GROUP) // 8):
            mine = iota((1, CAP, ND), 2) == iota((1, CAP, ND), 1) + opposite_set(number) * CAP
            lines = jnp.where(mine, ask_in[number * 8:number * 8 + 8], 0.0)
            wanted.append(jnp.sum(lines, axis=2, keepdims=True).reshape(8 * CAP, 1))
        wanted = jnp.concatenate(wanted, axis=0) - 1.0
        wrow[:, first * CAP:(first + GROUP) * CAP] = to_line(wanted)
        found = dot(one_hot(iota((GROUP * CAP, ROWS), 1) == wanted.astype(jnp.int32)), table[...])
        halves = [found[:, :256].reshape(GROUP, CAP, 256), found[:, 256:].reshape(GROUP, CAP, 256)]
        out1[first:first + GROUP] = jnp.concatenate(halves, axis=1).astype(BF16)
        for k in order_of(first):
            if k != HERE:
                remote(out1.at[k], recv1.at[opposite(k)], a_s, a_r, place(k)).start()
    recv1[HERE] = out1[HERE]

    @pl.when(away)
    def _():
        settle(v_held, ids_r.at[2])

    slot_line = v_held[0].astype(F32)
    slot_col = to_column(slot_line)
    loads[2].wait()
    loads[3].wait()

    settle(recv1.at[pl.ds(0, ND - 1)], a_r)
    embed = jnp.zeros((TOK, D), F32)
    for g in range(ND // GROUP):
        got = recv1[g * GROUP:(g + 1) * GROUP].astype(F32)
        rows = jnp.concatenate(
            [got[:, :CAP].reshape(GROUP * CAP, 256), got[:, CAP:].reshape(GROUP * CAP, 256)], axis=1
        ).astype(BF16)
        lanes = iota((TOK, GROUP * CAP), 1) + g * GROUP * CAP
        embed = embed + dot(one_hot(lanes == slot_col.astype(jnp.int32)), rows)
    emb[...] = embed.astype(BF16)
    center = jnp.mean(embed, -1, keepdims=True)
    deviation = embed - center
    inverse = lax.rsqrt(jnp.mean(deviation * deviation, -1, keepdims=True) + EPSILON)
    norm = deviation * inverse
    normed[...] = norm
    r_x[...] = inverse
    norm_low = norm.astype(BF16)

    for kind, (outbox, inbox) in enumerate(((out_q, q_s), (out_k, k_s), (out_v, v_s))):
        part = slice((kind + 1) * D, (kind + 2) * D)
        silu, slope = silu_parts(dot(norm_low, pw[:, part]))
        slopes[:, part] = slope
        low = silu.astype(BF16)
        for j in range(NC):
            outbox[j] = low[:, j * HD:(j + 1) * HD]
        inbox[block] = outbox[block]
    def hand_on(k):
        j = each_peer(k)
        for outbox, inbox in ((out_q, q_s), (out_k, k_s), (out_v, v_s)):
            remote(outbox.at[j], inbox.at[block], ex_s.at[k - 1], ex_r.at[k - 1], peer(j)).start()

    hand_on(1)
    hand_on(3)

    silu, slope = silu_parts(dot(norm_low, pw[:, :D]))
    slopes[:, :D] = slope
    gate_s[...] = silu.astype(BF16)

    def tile(qb, kb, diagonal):
        for part in range(TOK // QT):
            half = slice(part * QT, (part + 1) * QT)
            half_score = dot(q_s[qb, half, :], k_s[kb], 1, 1) * (0.5 * SCALE)
            t = jnp.tanh(half_score)
            turned = half_score * t
            weights = half_score + turned
            slope = (1.0 + t) * ((1.0 + half_score) - turned) * (0.5 * SCALE)
            if diagonal:
                allowed = (iota((QT, TOK), 1) - iota((QT, TOK), 0)) <= part * QT
                weights = jnp.where(allowed, weights, 0.0)
                slope = jnp.where(allowed, slope, 0.0)
            weights = weights.astype(BF16)
            w_t[tile_of(qb, kb), half, :] = weights
            d_t[tile_of(qb, kb), half, :] = slope.astype(BF16)
            if diagonal:
                att[qb, half, :] = dot(weights, v_s[kb])
            else:
                att[qb, half, :] += dot(weights, v_s[kb])

    def finish(qb):
        for part in range(TOK // QT):
            half = slice(part * QT, (part + 1) * QT)
            total = att[qb, half, :]
            mean = jnp.mean(total, -1, keepdims=True)
            out_off[qb, half, :] = (total - mean).astype(BF16)
            out_m[qb, :, half] = to_line(mean)

        @pl.when(qb != block)
        def _():
            remote(out_off.at[qb], off_s.at[:, pl.ds(head, HD)], ex_s.at[3], ex_r.at[3], peer(qb)).start()
            remote(out_m.at[qb], m_s.at[block], ex_s.at[4], ex_r.at[4], peer(qb)).start()

    after, across, ahead = rem(block + 1, NC), rem(block + 2, NC), rem(block + 3, NC)
    tile(block, block, True)
    settle(out_q.at[pl.ds(0, 3)], ex_s.at[0])
    settle(out_q.at[pl.ds(0, 3)], ex_s.at[2])
    hand_on(2)
    settle(q_s.at[pl.ds(0, 3)], ex_r.at[0])
    settle(q_s.at[pl.ds(0, 3)], ex_r.at[2])

    def diagonals(step, carry):
        b = rem(block + 1 + 2 * step, NC)
        tile(b, b, True)
        return carry

    def near_pairs(step, carry):
        one = jnp.where(step == 2, after, block)
        two = jnp.where(step == 0, after, ahead)
        tile(jnp.maximum(one, two), jnp.minimum(one, two), False)
        return carry

    lax.fori_loop(0, 2, diagonals, 0)
    lax.fori_loop(0, 3, near_pairs, 0)
    settle(q_s.at[pl.ds(0, 3)], ex_r.at[1])

    @pl.when(relay_away)
    def _():
        settle(og_mid, og_r.at[0])

    @pl.when(beyond_away)
    def _():
        remote(og_mid, og, og_s.at[1], og_r.at[1], device(held_x, y_at)).start()

    def near_rows(step, carry):
        qb = rem(block + 1 + 2 * step, NC)

        @pl.when(qb > across)
        def _():
            tile(qb, across, False)

        finish(qb)
        return carry

    lax.fori_loop(0, 2, near_rows, 0)
    tile(across, across, True)

    def far_row(kb, carry):
        tile(across, kb, False)
        return carry

    lax.fori_loop(0, across, far_row, 0)
    finish(across)

    @pl.when(block > across)
    def _():
        tile(block, across, False)

    finish(block)
    off_s[:, pl.ds(head, HD)] = out_off[block]
    m_s[block] = out_m[block]

    @pl.when(beyond_away)
    def _():
        settle(og, og_r.at[1])

    @pl.when(jnp.logical_not(beyond_away))
    def _():
        og[...] = og_mid[...]

    masked = jnp.where(slot_col >= 0.0, og[...], jnp.zeros((TOK, D), BF16))
    og[...] = masked
    gg[...] = dot(masked, ow[...], 1, 1)

    settle(off_s.at[:, pl.ds(0, 3 * HD)], ex_r.at[3])
    settle(m_s.at[pl.ds(0, 3)], ex_r.at[4])
    m_all = (m_s[0] + m_s[1] + m_s[2] + m_s[3]) * (1.0 / NC)
    for part in range(TOK // QT):
        half = slice(part * QT, (part + 1) * QT)
        off = off_s[half, :].astype(F32)
        gaps = [to_column((m_s[h] - m_all)[:, half]) for h in range(NC)]
        off = jnp.concatenate([off[:, h * HD:(h + 1) * HD] + gaps[h] for h in range(NC)], axis=1)
        deviation = off - jnp.mean(off, -1, keepdims=True)
        r_a = lax.rsqrt(jnp.mean(deviation * deviation, -1, keepdims=True) + EPSILON)
        a_norm = deviation * r_a
        an_s[half, :] = a_norm
        cot = gg[half, :] * gate_s[half, :].astype(F32)
        grad = r_a * (
            cot - jnp.mean(cot, -1, keepdims=True) - a_norm * jnp.mean(cot * a_norm, -1, keepdims=True)
        )
        grad = grad.astype(BF16)
        for j in range(NC):
            out_da[j, half, :] = grad[:, j * HD:(j + 1) * HD]
        for k in range(1, NC):
            j = each_peer(k)
            rows = pl.ds(part * QT, QT)
            remote(out_da.at[j, rows], da_s.at[block, rows], ex_s.at[5], ex_r.at[5], peer(j)).start()
    da_s[block] = out_da[block]

    a_norm = an_s[...]
    gated = (a_norm * gate_s[...].astype(F32)).astype(BF16)
    mix[...] = (emb[...].astype(F32) + dot(gated, ow[...])).astype(BF16)

    @pl.when(away)
    def _():
        remote(mix, mixed, mx_s, mx_r, device(held_x, held_y)).start()

    @pl.when(jnp.logical_not(away))
    def _():
        mixed[...] = mix[...]

    e_acc[...] = dot((gg[...] * a_norm * slopes[:, :D]).astype(BF16), pw[:, :D], 1, 1)
    for b in range(NC):
        q_t[b] = q_s[b].astype(F32).T.astype(BF16)

    def by_row(qb):
        grad = da_s[qb]
        dq_acc[...] = jnp.zeros((TOK, HD), F32)

        def tile(kb, carry):
            slope = dot(grad, v_s[kb], 1, 1)
            ds = (slope * d_t[tile_of(qb, kb)].astype(F32)).astype(BF16)
            d_t[tile_of(qb, kb)] = ds
            dq_acc[...] += dot(ds, k_s[kb])
            return carry

        lax.fori_loop(0, qb + 1, tile, 0)
        out_dq[qb] = dq_acc[...].astype(BF16)
        da_t[qb] = grad.astype(F32).T.astype(BF16)

    by_row(block)
    settle(da_s.at[pl.ds(0, 3)], ex_r.at[5])

    def other_row(k, carry):
        qb = each_peer(k)
        by_row(qb)
        remote(out_dq.at[qb], dqkv.at[:, pl.ds(head, HD)], ex_s.at[6], ex_r.at[6], peer(qb)).start()
        return carry

    lax.fori_loop(1, NC, other_row, 0)

    def by_column(step, carry):
        kb = rem(block + jnp.where(step < 2, 2 - step, step + 1), NC)
        d_kv[...] = jnp.zeros((2, HD, TOK), F32)

        def tile(qb, inner):
            d_kv[0] += dot(q_t[qb], d_t[tile_of(qb, kb)])
            d_kv[1] += dot(da_t[qb], w_t[tile_of(qb, kb)])
            return inner

        lax.fori_loop(kb, NC, tile, 0)
        out_dk[kb] = d_kv[0].T.astype(BF16)
        out_dv[kb] = d_kv[1].T.astype(BF16)

        @pl.when(kb != block)
        def _():
            remote(out_dk.at[kb], dqkv.at[:, pl.ds(D + head, HD)], ex_s.at[7], ex_r.at[7], peer(kb)).start()
            remote(out_dv.at[kb], dqkv.at[:, pl.ds(2 * D + head, HD)], ex_s.at[8], ex_r.at[8], peer(kb)).start()

        return carry

    lax.fori_loop(0, NC, by_column, 0)
    dqkv[:, pl.ds(head, HD)] = out_dq[block]
    dqkv[:, pl.ds(D + head, HD)] = out_dk[block]
    dqkv[:, pl.ds(2 * D + head, HD)] = out_dv[block]

    incoming = e_acc[...]
    for kind, part in ((6, 0), (7, 1), (8, 2)):
        settle(off_s.at[:, pl.ds(0, 3 * HD)], ex_r.at[kind])
        grad = dqkv[:, part * D:(part + 1) * D].astype(F32) * slopes[:, (part + 1) * D:(part + 2) * D]
        incoming = incoming + dot(grad.astype(BF16), pw[:, (part + 1) * D:(part + 2) * D], 1, 1)
    norm = normed[...]
    embed_grad = r_x[...] * (
        incoming
        - jnp.mean(incoming, -1, keepdims=True)
        - norm * jnp.mean(incoming * norm, -1, keepdims=True)
    ) + og[...].astype(F32)
    embed_grad = embed_grad.astype(BF16)

    for first in range(0, ND, GROUP):
        slots = iota((GROUP * CAP, TOK), 0) + first * CAP
        sorted_rows = dot(one_hot(slots == slot_line.astype(jnp.int32)), embed_grad)
        halves = [sorted_rows[:, :256].reshape(GROUP, CAP, 256), sorted_rows[:, 256:].reshape(GROUP, CAP, 256)]
        out2[first:first + GROUP] = jnp.concatenate(halves, axis=1).astype(BF16)
        for k in order_of(first):
            if k != HERE:
                remote(out2.at[k], recv2.at[opposite(k)], b_s, b_r, place(k)).start()
    recv2[HERE] = out2[HERE]

    @pl.when(relay_away)
    def _():
        settle(ask_mid, ids_s.at[0])

    @pl.when(jnp.logical_not(relay_away))
    def _():
        settle(ask_mid.at[pl.ds(0, 7)], ids_s.at[0])

    settle(ask_in.at[pl.ds(0, 120)], ids_s.at[1])
    settle(out1.at[pl.ds(0, ND - 1)], a_s)
    for kind in (1, 3, 5, 6, 7, 8):
        settle(out_q.at[pl.ds(0, 3)], ex_s.at[kind])
    settle(out_m.at[pl.ds(0, 3)], ex_s.at[4])

    @pl.when(relay_away)
    def _():
        settle(og_in, og_s.at[0])

    @pl.when(beyond_away)
    def _():
        settle(og_mid, og_s.at[1])

    @pl.when(away)
    def _():
        settle(v_out, ids_s.at[2])
        settle(mix, mx_s)
        settle(mixed, mx_r)

    settle(out2.at[pl.ds(0, ND - 1)], b_s)
    settle(recv2.at[pl.ds(0, ND - 1)], b_r)


def scatter_kernel(wrow, recv2_h, mix, out, mixed, rows, recv2, load):
    step = pl.program_id(0)

    @pl.when(step == 0)
    def _():
        copies = []
        for g in range(ND // GROUP):
            part = pl.ds(g * GROUP, GROUP)
            copies.append(pltpu.make_async_copy(recv2_h.at[part], recv2.at[part], load.at[g]))
            copies[g].start()
        for g in range(ND // GROUP):
            copies[g].wait()
            got = recv2[g * GROUP:(g + 1) * GROUP].astype(F32)
            rows[g * GROUP * CAP:(g + 1) * GROUP * CAP] = jnp.concatenate(
                [got[:, :CAP].reshape(GROUP * CAP, 256), got[:, CAP:].reshape(GROUP * CAP, 256)], axis=1
            ).astype(BF16)

    mixed[...] = mix[...]
    size = out.shape[0]
    wanted = wrow[...].astype(jnp.int32) - step * size
    for part in range(size // 256):
        at = slice(part * 256, (part + 1) * 256)
        out[at, :] = dot(one_hot(iota((256, SLOTS), 0) + part * 256 == wanted), rows[...])


def shards(owner, row, lengths, table, proj_weight, out_weight, out_grad):
    vmem = pl.BlockSpec(memory_space=pltpu.VMEM)
    hbm = pl.BlockSpec(memory_space=pltpu.HBM)
    V = pltpu.VMEM
    DMA = pltpu.SemaphoreType.DMA
    mixed, recv2, wrow = pl.pallas_call(
        layer,
        out_shape=(
            jax.ShapeDtypeStruct((TOK, D), BF16),
            jax.ShapeDtypeStruct((ND, 2 * CAP, 256), BF16),
            jax.ShapeDtypeStruct((1, SLOTS), F32),
        ),
        in_specs=[hbm, hbm, pl.BlockSpec(memory_space=pltpu.SMEM), hbm, hbm, hbm, hbm],
        out_specs=(vmem, vmem, vmem),
        scratch_shapes=[
            V((1, TOK), jnp.int32), V((1, TOK), jnp.int32), V((ROWS, D), BF16), V((D, 4 * D), BF16), V((D, D), BF16), V((TOK, D), BF16), V((TOK, D), BF16), V((TOK, D), BF16),
            V((1, 1, TOK), jnp.int32), V((1, 1, TOK), jnp.int32), V((8, 1, ND), F32), V((8, 1, ND), F32), V((ND, 1, ND), F32),
            V((ND, 2 * CAP, 256), BF16), V((ND, 2 * CAP, 256), BF16), V((TOK, D), BF16),
            V((TOK, D), F32), V((TOK, 1), F32), V((TOK, 4 * D), F32), V((TOK, D), BF16), V((TOK, D), F32),
        ] + [V((NC, TOK, HD), BF16)] * 12 + [
            V((TOK, D), BF16), V((TOK, 3 * D), BF16), V((NC, 1, TOK), F32), V((NC, 1, TOK), F32),
            V((TOK, D), F32), V((NC, TOK, HD), F32), V((10, TOK, TOK), BF16), V((10, TOK, TOK), BF16),
            V((NC, HD, TOK), BF16), V((NC, HD, TOK), BF16),
            V((TOK, HD), F32), V((2, HD, TOK), F32), V((TOK, D), F32), V((TOK, D), BF16),
            V((ND, 2 * CAP, 256), BF16),
            DMA((6,)), DMA((3,)), DMA((3,)), DMA((2,)), DMA((2,)), DMA, DMA, DMA((9,)), DMA((9,)), DMA, DMA, DMA, DMA,
        ],
        compiler_params=pltpu.CompilerParams(
            collective_id=0, has_side_effects=True, vmem_limit_bytes=63 * 1024 * 1024
        ),
    )(
        owner.reshape(1, TOK), row.reshape(1, TOK), lengths, table, proj_weight, out_weight,
        out_grad.reshape(TOK, D),
    )
    steps = 4
    table_grad, mixed = pl.pallas_call(
        scatter_kernel,
        grid=(steps,),
        out_shape=(jax.ShapeDtypeStruct((ROWS, D), F32), jax.ShapeDtypeStruct((TOK, D), BF16)),
        in_specs=[vmem, hbm, pl.BlockSpec((TOK // steps, D), lambda i: (i, 0))],
        out_specs=(
            pl.BlockSpec((ROWS // steps, D), lambda i: (i, 0)),
            pl.BlockSpec((TOK // steps, D), lambda i: (i, 0)),
        ),
        scratch_shapes=[V((SLOTS, D), BF16), V((ND, 2 * CAP, 256), BF16), DMA((ND // GROUP,))],
        compiler_params=pltpu.CompilerParams(vmem_limit_bytes=63 * 1024 * 1024),
    )(wrow, recv2, mixed)
    return (mixed.reshape(1, TOK, D), table_grad)


def solution(mesh):
    placed = (
        P("user", "ctx", None),
        P("user", "ctx"),
        P("user"),
        P(("user", "ctx"), None),
        P(),
        P(),
        P("user", "ctx", None),
    )
    return jax.shard_map(
        shards,
        mesh=mesh,
        in_specs=placed,
        out_specs=(P("user", "ctx", None), P(("user", "ctx"), None)),
        check_vma=False,
    )
```
